128 devices in a mesh: dp: 16 (over z_hi, y, core), tensor: 8 (over x, z_lo).
Axes of the slice: x: 4, y: 4, z: 4 (z_hi: 2, z_lo: 2; z = z_hi * 2 + z_lo), core: 2. Of those that a mesh axis runs over, the one named last changes fastest.
Arguments:
- x_states: bfloat16 [48, 192, 8192], P('dp'), may hold values from -6 to 6
- mask_bits: int32 [48, 192], P('dp'), may hold values 0 or 1
- prompt_len: int32 [48], P('dp'), may hold values from 24 to 95
- weight: bfloat16 [8192, 8192], P(None, 'tensor'), may hold values from -0.0625 to 0.0625
- norm_gain: float32 [8192], replicated, may hold values from 0.1 to 1.9
- mask_embed: bfloat16 [8192], replicated, may hold values from -6 to 6
- grads: float32 [16, 2, 64, 8192], P('dp', None, None, 'tensor'), may hold values from -6 to 6
- factors: float32 [2, 64, 8192], P(None, None, 'tensor'), may hold values from -0.15625 to 0.15625
- first_moment: float32 [2, 64, 8192], P(None, None, 'tensor'), may hold values from -6 to 6
- second_moment: float32 [2, 64, 8192], P(None, None, 'tensor'), may hold values from 0.25 to 4
Outputs:
- denoised: bfloat16 [48, 192, 8192], P('dp', None, 'tensor')
- new_first: float32 [2, 64, 8192], P(None, 'dp', 'tensor')
- new_second: float32 [2, 64, 8192], P(None, 'dp', 'tensor')
The draws below stay inside these ranges and needn't reach their ends.
All inputs are finite; a program needn't handle non-finite values. No bound on the sum of `mask_bits` on one device may be relied on, other than what follows from the above.
Results may differ from the reference program's by a relative error of at most 0.0095.
Values may be sent and summed in bfloat16 or wider, within the bound.
No kernel may reach another device: no remote copies, remote signals or barrier semaphores. Data moves between devices by JAX's collectives and lax.ppermute only.
A program may use at most 192 MiB of HBM per device.

```python
import math
import jax
import jax.numpy as jnp
from jax import lax

D = 8192
R = 64
LEN = 192
SEQS = 48
LEARNERS = 16


def place_ends(array, key, least, high):
    extent = array.shape
    index_at = [jax.random.randint(jax.random.fold_in(key, axis), (), 0, extent[axis]) for axis in range(len(extent))]
    array = array.at[tuple(index_at)].set(least)
    longest = extent.index(max(extent))
    index_at[longest] = (index_at[longest] + 1) % extent[longest]
    return array.at[tuple(index_at)].set(high)


def spiked(drawn, own_key, source, target, shards_of, factor):
    def block_of(dim):
        return (jnp.arange(drawn.shape[dim]) // (drawn.shape[dim] // shards_of)).reshape((-1,) + (1,) * (drawn.ndim - 1 - dim))

    near = jax.random.permutation(own_key, shards_of)[block_of(target)]
    far = (block_of(target) + shards_of // 2) % shards_of
    return jnp.where((block_of(source) == near) | (block_of(source) == far), factor * drawn, drawn)


def levels(own_key, dims, cuts, low, largest):
    level = 1.0
    for axis_at, blocks in cuts:
        steps = jax.random.uniform(jax.random.fold_in(jax.random.fold_in(own_key, 6), axis_at), (blocks,), jnp.float32, low / len(cuts), largest / len(cuts))
        level = level * jnp.repeat(jnp.exp(steps), dims[axis_at] // blocks).reshape((-1,) + (1,) * (len(dims) - 1 - axis_at))
    return level


def noise(rng, shape, spread, most, shards=(), held_as=jnp.bfloat16):
    loudness = levels(rng, shape, shards, -0.22, 0.18) if shards else 1.0
    drawn = jax.random.normal(rng, shape, jnp.float32) * spread * loudness
    return jnp.minimum(jnp.maximum(drawn, -most), most).astype(held_as)


def heavy_noise(key, shape, scale, limit, cuts, heavy, kind=jnp.bfloat16):
    drawn = scale * jax.random.normal(key, shape, jnp.float32)
    if cuts:
        drawn = drawn * levels(key, shape, cuts, -0.22, 0.18)
    return jnp.clip(spiked(drawn, jax.random.fold_in(key, 3), *heavy), -limit, limit).astype(kind)


def setup_inputs(seed: int = 0) -> dict:
    seeds = jax.random.split(jax.random.key(seed), 11)
    return {
        "x_states": noise(seeds[0], (SEQS, LEN, D), 1.0, 6.0, ((0, 16),)),
        "mask_bits": place_ends((jax.random.randint(seeds[1], (SEQS, LEN), 0, 2) < 1).astype(jnp.int32), jax.random.fold_in(seeds[1], 1), 0, 1),
        "prompt_len": place_ends(jax.random.randint(seeds[2], (SEQS,), LEN // 8, LEN // 2), jax.random.fold_in(seeds[2], 1), LEN // 8, (LEN // 2) - 1).astype(jnp.int32),
        "weight": noise(seeds[3], (D, D), D ** -0.5, 0.0625, ((1, 8),)),
        "norm_gain": jnp.clip(1.0 + 0.18 * jax.random.normal(seeds[4], (D,), jnp.float32), 0.1, 1.9),
        "mask_embed": noise(seeds[5], (D,), 1.0, 6.0),
        "grads": heavy_noise(seeds[6], (LEARNERS, 2, R, D), 1.0, 6.0, ((0, 16), (3, 8)), (0, 2, 16, 2.0), jnp.float32),
        "factors": noise(seeds[7], (2, R, D), (D // 8 + 8 * R) ** -0.5, 0.15625, ((2, 8),), jnp.float32),
        "first_moment": noise(seeds[8], (2, R, D), 1.0, 6.0, ((2, 8),), jnp.float32),
        "second_moment": jnp.clip(jnp.exp(math.log(4.0) - 2.7725887 * jax.random.uniform(seeds[9], (2, R, D), jnp.float32) ** levels(seeds[9], (2, R, D), ((2, 8),), -0.2, 0.2)), 0.25, 4.0),
    }


beta_one = 0.9
beta_two = 0.999
learn_rate = 0.03
adam_count = 100
epsilon = 1e-08
adapter_scale = 2.0
norm_epsilon = 1e-05

def adam_update(summed_grad, first_moment, second_moment, param_rows):
    new_first = beta_one * first_moment + (1.0 - beta_one) * summed_grad
    new_second = beta_two * second_moment + (1.0 - beta_two) * summed_grad * summed_grad
    step_size = learn_rate / (1.0 - beta_one ** adam_count)
    divisor = jnp.sqrt(new_second / (1.0 - beta_two ** adam_count)) + epsilon
    return (new_first, new_second, param_rows - step_size * new_first / divisor)

def prepare(x_states, mask_bits, prompt_len, norm_gain, mask_embed):
    length = x_states.shape[1]
    position = jnp.arange(length, dtype=jnp.int32)
    response = position[None, :] >= prompt_len[:, None]
    masked = jnp.logical_and(response, mask_bits == 1)
    hidden = jnp.where(masked[:, :, None], mask_embed[None, None, :], x_states)
    widened = hidden.astype(jnp.float32)
    norm_scale = lax.rsqrt(lax.optimization_barrier(jnp.mean(widened * widened, axis=-1, keepdims=True)) + norm_epsilon)
    normed = (widened * norm_gain).astype(jnp.bfloat16)
    return (response, widened, norm_scale, normed.reshape(-1, x_states.shape[2]))

def finish(x_states, response, widened, norm_scale, projected_states, col_start):
    seq_count = x_states.shape[0]
    length = x_states.shape[1]
    col_width = projected_states.shape[1]
    projected_states = projected_states.reshape(seq_count, length, col_width) * norm_scale
    own_part = lax.dynamic_slice_in_dim(widened, col_start, col_width, 2)
    kept = lax.dynamic_slice_in_dim(x_states, col_start, col_width, 2).astype(jnp.float32)
    return jnp.where(response[:, :, None], own_part + projected_states, kept).astype(jnp.bfloat16)

def reference(x_states, mask_bits, prompt_len, weight, norm_gain, mask_embed, grads, factors, first_moment, second_moment):
    summed_grad = lax.optimization_barrier(jnp.sum(grads, axis=0))
    new_first, new_second, updated = adam_update(summed_grad, first_moment, second_moment, factors)
    transferred_factors = updated.astype(jnp.bfloat16)
    response, widened, norm_scale, normed = prepare(x_states, mask_bits, prompt_len, norm_gain, mask_embed)
    frozen_weight_term = jnp.dot(normed, weight, preferred_element_type=jnp.float32)
    rank_factor_product = lax.dot_general(normed, transferred_factors[1], (((1,), (1,)), ((), ())), preferred_element_type=jnp.float32)
    adapter_term = jnp.dot(rank_factor_product, transferred_factors[0].astype(jnp.float32), precision=lax.Precision.HIGHEST)
    projected_states = frozen_weight_term + adapter_scale * adapter_term
    denoised = finish(x_states, response, widened, norm_scale, projected_states, 0)
    return (denoised, new_first, new_second)
```

```python
import functools
import itertools

import jax
import jax.numpy as jnp
from jax import lax
from jax.experimental import pallas as pl
from jax.experimental.pallas import tpu as pltpu
from jax.sharding import Mesh, PartitionSpec as P

beta_one = 0.9
beta_two = 0.999
learn_rate = 0.03
adam_count = 100
epsilon = 1e-08
adapter_scale = 2.0
norm_epsilon = 1e-05

SIZES = {"zh": 2, "y": 4, "c": 2, "x": 4, "zl": 2}
DP = ("zh", "y", "c")
TENSOR = ("x", "zl")
KB = 512
MIB = 1 << 20


def f32(v):
    return v.astype(jnp.float32)


def bf16(v):
    return v.astype(jnp.bfloat16)


def exchange(v, axes, key):
    ids = list(itertools.product(*[range(SIZES[a]) for a in axes]))
    index = {t: i for i, t in enumerate(ids)}
    pairs = [(index[t], index[tuple(a ^ k for a, k in zip(t, key))]) for t in ids]
    return lax.ppermute(v, tuple(axes), pairs)


def adam_update(summed_grad, first_moment, second_moment):
    new_first = beta_one * first_moment + (1.0 - beta_one) * summed_grad
    new_second = beta_two * second_moment + (1.0 - beta_two) * summed_grad * summed_grad
    return new_first, new_second


def factor_update(new_first, new_second, param_rows):
    step_size = learn_rate / (1.0 - beta_one**adam_count)
    divisor = jnp.sqrt(new_second / (1.0 - beta_two**adam_count)) + epsilon
    return param_rows - step_size * new_first / divisor


def main_kernel(first, x_ref, mask_ref, gain_ref, embed_ref, w_ref, *rest):
    if first:
        _, acc_ref, sq_ref = rest
    else:
        _, acc_in, sq_in, acc_ref, sq_ref = rest
    step = pl.program_id(0)
    rows = acc_ref.shape[0]
    masked = mask_ref[...] > 0.0
    states = x_ref[...].reshape(rows, KB).astype(jnp.float32)
    hidden = jnp.where(masked, embed_ref[...].astype(jnp.float32), states)
    normed = (hidden * gain_ref[...]).astype(jnp.bfloat16)
    squares = hidden * hidden
    part = squares[:, 0:128]
    for j in range(1, KB // 128):
        part = part + squares[:, j * 128 : (j + 1) * 128]
    product = jnp.dot(normed, w_ref[...], preferred_element_type=jnp.float32)

    if first:

        @pl.when(step == 0)
        def _():
            acc_ref[...] = product
            sq_ref[...] = part

        @pl.when(step > 0)
        def _():
            acc_ref[...] += product
            sq_ref[...] += part
    else:

        @pl.when(step == 0)
        def _():
            acc_ref[...] = acc_in[...] + product
            sq_ref[...] = sq_in[...] + part

        @pl.when(step > 0)
        def _():
            acc_ref[...] += product
            sq_ref[...] += part


def main_chunk(x, mask, gain, embed, w, token, state, start, stop):
    seqs, length, width = x.shape
    rows = seqs * length
    cols = w.shape[1]
    first = state is None
    k0 = start // KB
    steps = (stop - start) // KB
    whole = pl.BlockSpec(memory_space=pltpu.VMEM)
    in_specs = [
        pl.BlockSpec((seqs, length, KB), lambda i: (0, 0, k0 + i)),
        whole,
        pl.BlockSpec((1, KB), lambda i: (0, k0 + i)),
        pl.BlockSpec((1, KB), lambda i: (0, k0 + i)),
        pl.BlockSpec((KB, cols), lambda i: (k0 + i, 0)),
        pl.BlockSpec(memory_space=pl.ANY),
    ]
    args = [x, mask, gain, embed, w, token]
    aliases = {}
    if not first:
        in_specs += [whole, whole]
        args += list(state)
        aliases = {6: 0, 7: 1}
    return pl.pallas_call(
        functools.partial(main_kernel, first),
        grid=(steps,),
        in_specs=in_specs,
        out_specs=[whole, whole],
        out_shape=[
            jax.ShapeDtypeStruct((rows, cols), jnp.float32),
            jax.ShapeDtypeStruct((rows, 128), jnp.float32),
        ],
        input_output_aliases=aliases,
        compiler_params=pltpu.CompilerParams(vmem_limit_bytes=28 * MIB),
        cost_estimate=pl.CostEstimate(
            flops=2 * rows * (stop - start) * cols,
            bytes_accessed=2 * (stop - start) * (rows + cols),
            transcendentals=0,
        ),
        name="main_chunk",
    )(*args)


def low_rank_kernel(own_ref, other_ref, bown_ref, bother_ref, out_ref):
    half = own_ref.shape[0] // 2
    dims = (((1,), (1,)), ((), ()))
    prod = lax.dot_general(own_ref[...], bown_ref[...], dims, preferred_element_type=jnp.float32)
    prod += lax.dot_general(other_ref[...], bother_ref[...], dims, preferred_element_type=jnp.float32)
    out_ref[...] = jnp.concatenate([prod[:half], prod[half:]], axis=1).astype(jnp.bfloat16)


def low_rank(own, other, b_own, b_other):
    rows = own.shape[0]
    rank = b_own.shape[0]
    return pl.pallas_call(
        low_rank_kernel,
        out_shape=jax.ShapeDtypeStruct((rows // 2, 2 * rank), jnp.bfloat16),
        compiler_params=pltpu.CompilerParams(vmem_limit_bytes=8 * MIB),
        name="low_rank",
    )(own, other, b_own, b_other)


def final_kernel(
    mine_ref, r1_ref, r2_ref, r3_ref, a_ref, acc_ref, sq_ref, xs_ref, mask_ref, resp_ref, embed_ref, out_ref
):
    rows = acc_ref.shape[0]
    half = rows // 2
    rank = a_ref.shape[0]
    total = mine_ref[...].astype(jnp.float32) + r1_ref[...].astype(jnp.float32)
    total += r2_ref[...].astype(jnp.float32) + r3_ref[...].astype(jnp.float32)
    total = total.astype(jnp.bfloat16)
    mean = jnp.sum(sq_ref[...], axis=1, keepdims=True) * (1.0 / 8192.0)
    scale = lax.rsqrt(mean + norm_epsilon)
    for piece in range(2):
        low = total[:, piece * rank : (piece + 1) * rank]
        adapter = jnp.dot(low, a_ref[...], preferred_element_type=jnp.float32)
        at = slice(piece * half, (piece + 1) * half)
        states = xs_ref[at, :].astype(jnp.float32)
        hidden = jnp.where(mask_ref[at, :] > 0.0, embed_ref[...].astype(jnp.float32), states)
        projected = (acc_ref[at, :] + adapter_scale * adapter) * scale[at]
        value = jnp.where(resp_ref[at, :] > 0.0, hidden + projected, states).astype(jnp.bfloat16)
        out_ref[at, :] = value


def final(mine, received, a, acc, sq, xs, mask, resp, embed):
    rows, cols = acc.shape
    return pl.pallas_call(
        final_kernel,
        out_shape=jax.ShapeDtypeStruct((rows, cols), jnp.bfloat16),
        compiler_params=pltpu.CompilerParams(vmem_limit_bytes=20 * MIB),
        name="final",
    )(mine, *received, a, acc, sq, xs, mask, resp, embed)


def local(x, mask_bits, prompt_len, weight, norm_gain, mask_embed, grads, factors, first_moment, second_moment):
    seqs, length, width = x.shape
    rows = seqs * length
    cols = weight.shape[1]
    half = cols // 2
    core = lax.axis_index("c")
    col_start = lax.axis_index(TENSOR) * cols
    rank = factors.shape[1]
    share = rank // 16

    def own_half(v):
        return lax.dynamic_slice_in_dim(v, core * half, half, v.ndim - 1)

    def other_half(v):
        return lax.dynamic_slice_in_dim(v, (1 - core) * half, half, v.ndim - 1)

    grad = grads[0]
    from_core = exchange(bf16(other_half(grad)), "c", (1,))
    total = own_half(grad) + f32(from_core)
    sent = bf16(total)
    from_y = [exchange(sent, "y", (k,)) for k in (2, 3, 1)]
    total = total + f32(from_y[0]) + f32(from_y[1]) + f32(from_y[2])
    from_z = exchange(bf16(total), ("zh",), (1,))
    total = total + f32(from_z)

    new_first, new_second = adam_update(total, own_half(first_moment), own_half(second_moment))
    shipped = bf16(factor_update(new_first, new_second, own_half(factors)))
    b_own = shipped[1]
    b_other = exchange(b_own, "c", (1,))
    a_own = shipped[0]
    a_other = exchange(a_own, "c", (1,))

    my_row = lax.axis_index(DP) * share
    pair_row = (lax.axis_index(DP) + 1 - 2 * core) * share
    rows_out = lax.dynamic_slice_in_dim(total, pair_row, share, 1)
    rows_in = exchange(rows_out, "c", (1,))
    rows_mine = lax.dynamic_slice_in_dim(total, my_row, share, 1)

    def ordered(mine, others):
        return jnp.where(
            core == 0, jnp.concatenate([mine, others], -1), jnp.concatenate([others, mine], -1)
        )

    row_total = ordered(rows_mine, rows_in)
    out_first, out_second = adam_update(
        row_total,
        lax.dynamic_slice_in_dim(first_moment, my_row, share, 1),
        lax.dynamic_slice_in_dim(second_moment, my_row, share, 1),
    )

    position = jnp.arange(length, dtype=jnp.int32)
    response = position[None, :] >= prompt_len[:, None]
    masked = jnp.logical_and(response, mask_bits == 1)
    mask_col = f32(masked).reshape(rows, 1)
    resp_col = f32(response).reshape(rows, 1)
    xs = lax.dynamic_slice_in_dim(x, col_start, cols, 2).reshape(rows, cols)
    embed_cols = lax.dynamic_slice_in_dim(mask_embed, col_start, cols, 0)
    gain_cols = lax.dynamic_slice_in_dim(norm_gain, col_start, cols, 0)
    normed_cols = bf16(f32(jnp.where(masked.reshape(rows, 1), embed_cols[None, :], xs)) * gain_cols[None, :])
    gain = norm_gain.reshape(1, width)
    embed = mask_embed.reshape(1, width)

    state = main_chunk(x, mask_col, gain, embed, weight, from_core, None, 0, width // 2)
    state = main_chunk(x, mask_col, gain, embed, weight, from_y[0], state, width // 2, 3 * width // 4)

    low = low_rank(own_half(normed_cols), other_half(normed_cols), b_own, b_other)
    from_zl = exchange(low, ("zl",), (1,))
    state = main_chunk(x, mask_col, gain, embed, weight, b_other, state, 3 * width // 4, 7 * width // 8)
    low = bf16(f32(low) + f32(from_zl))
    from_x = [exchange(low, ("x",), (k,)) for k in (2, 3, 1)]
    state = main_chunk(x, mask_col, gain, embed, weight, from_zl, state, 7 * width // 8, width)
    a_full = ordered(a_own, a_other)
    out = final(low, from_x, a_full, *state, xs, mask_col, resp_col, embed_cols.reshape(1, cols))
    return out.reshape(seqs, length, cols), out_first, out_second


def solution(mesh):
    split = Mesh(mesh.devices.reshape(2, 4, 2, 4, 2), ("zh", "y", "c", "x", "zl"))
    placed = (
        P(DP, None, None),
        P(DP, None),
        P(DP),
        P(None, TENSOR),
        P(),
        P(),
        P(DP, None, None, TENSOR),
        P(None, None, TENSOR),
        P(None, None, TENSOR),
        P(None, None, TENSOR),
    )
    return jax.shard_map(
        local,
        mesh=split,
        in_specs=placed,
        out_specs=(P(DP, None, TENSOR), P(None, DP, TENSOR), P(None, DP, TENSOR)),
        check_vma=False,
    )
```

```python
import functools
import itertools

import jax
import jax.numpy as jnp
from jax import lax
from jax.experimental import pallas as pl
from jax.experimental.pallas import tpu as pltpu
from jax.sharding import Mesh, PartitionSpec as P

beta_one = 0.9
beta_two = 0.999
learn_rate = 0.03
adam_count = 100
epsilon = 1e-08
adapter_scale = 2.0
norm_epsilon = 1e-05

SIZES = {"zh": 2, "y": 4, "c": 2, "x": 4, "zl": 2}
DP = ("zh", "y", "c")
TENSOR = ("x", "zl")
UNIT = 1024
FEATURES = 8192
MIN_PROMPT = 24
SKIP = 16
MIB = 1 << 20


def f32(v):
    return v.astype(jnp.float32)


def bf16(v):
    return v.astype(jnp.bfloat16)


def exchange(v, axes, key):
    ids = list(itertools.product(*[range(SIZES[a]) for a in axes]))
    index = {t: i for i, t in enumerate(ids)}
    pairs = [(index[t], index[tuple(a ^ k for a, k in zip(t, key))]) for t in ids]
    return lax.ppermute(v, tuple(axes), pairs)


def adam_update(summed_grad, first_moment, second_moment):
    new_first = beta_one * first_moment + (1.0 - beta_one) * summed_grad
    new_second = beta_two * second_moment + (1.0 - beta_two) * summed_grad * summed_grad
    return new_first, new_second


def factor_update(new_first, new_second, param_rows):
    step_size = learn_rate / (1.0 - beta_one**adam_count)
    divisor = jnp.sqrt(new_second / (1.0 - beta_two**adam_count)) + epsilon
    return param_rows - step_size * new_first / divisor


def hidden_block(x_ref, lead, mask_ref, embed, seq, lanes):
    states = x_ref[lead + (seq, slice(None), lanes)].astype(jnp.float32)[MIN_PROMPT - SKIP :]
    return jnp.where(mask_ref[seq] > 0.0, embed, states)


def normalise(x_ref, unit, mask_ref, gain_ref, embed_ref, k0, normed_ref, sq_ref, first):
    seqs, kept, _ = mask_ref.shape
    for seq in range(seqs):
        rows = slice(seq * kept, (seq + 1) * kept)
        squares = None if first else sq_ref[rows]
        for j in range(UNIT // 128):
            at = slice(k0 + j * 128, k0 + (j + 1) * 128)
            hidden = hidden_block(x_ref, (unit,), mask_ref, embed_ref[:, at], seq, slice(j * 128, (j + 1) * 128))
            squares = hidden * hidden if squares is None else squares + hidden * hidden
            normed_ref[rows, j * 128 : (j + 1) * 128] = (hidden * gain_ref[:, at]).astype(jnp.bfloat16)
        sq_ref[rows] = squares


def fetch(x_ref, w_ref, unit, x_dst, w_dst, slot, sem):
    k0 = unit * UNIT
    return [
        pltpu.make_async_copy(w_ref.at[pl.ds(k0, UNIT)], w_dst.at[slot], sem.at[0]),
        pltpu.make_async_copy(
            x_ref.at[:, pl.ds(SKIP, x_ref.shape[1] - SKIP), pl.ds(k0, UNIT)], x_dst.at[slot], sem.at[1]
        ),
    ]


def multiply(units, blocks, mask_ref, gain_ref, embed_ref, acc_ref, sq_ref, normed, fresh):
    def ready(i):
        x_buf, _, slot, copies = blocks[i]
        for copy in copies:
            copy.wait()
        normalise(
            x_buf, slot, mask_ref, gain_ref, embed_ref, units[i] * UNIT, normed[i % 2], sq_ref, fresh and i == 0
        )

    ready(0)
    for i in range(len(units)):
        if i + 1 < len(units):
            ready(i + 1)
        _, w_buf, slot, _ = blocks[i]
        product = jnp.dot(normed[i % 2][...], w_buf[slot], preferred_element_type=jnp.float32)
        if fresh and i == 0:
            acc_ref[...] = product
        else:
            acc_ref[...] += product


def head_kernel(
    units, following, place_ref, prompt_ref, bits_ref, gain_ref, embed_ref, x_ref, w_ref, _,
    acc_ref, sq_ref, mask_ref, own_ref, xs_ref, x_next, w_next,
    x_buf, w_buf, normed_a, normed_b, sems, own_sem,
):
    seqs, kept, _ = mask_ref.shape
    cols = own_ref.shape[1]
    col = pl.multiple_of(place_ref[0], cols)
    own = pltpu.make_async_copy(x_ref.at[:, :, pl.ds(col, cols)], xs_ref, own_sem)
    own.start()
    blocks = []
    for i, unit in enumerate(units):
        copies = fetch(x_ref, w_ref, unit, x_buf, w_buf, i, sems.at[i])
        for copy in copies:
            copy.start()
        blocks.append((x_buf, w_buf, i, copies))
    after = []
    for i, unit in enumerate(following):
        after += fetch(x_ref, w_ref, unit, x_next, w_next, i, sems.at[len(units) + i])
    for copy in after:
        copy.start()

    length = bits_ref.shape[1]
    here = lax.broadcasted_iota(jnp.int32, (kept, length), 0) + MIN_PROMPT
    there = lax.broadcasted_iota(jnp.int32, (kept, length), 1)
    for seq in range(seqs):
        chosen = jnp.logical_and(here == there, here >= prompt_ref[seq])
        bits = jnp.where(chosen, bits_ref[seq : seq + 1, :], 0)
        column = jnp.sum((bits == 1).astype(jnp.float32), axis=1, keepdims=True)
        mask_ref[seq] = jnp.broadcast_to(column, (kept, 128))

    own.wait()
    for seq in range(seqs):
        rows = slice(seq * kept, (seq + 1) * kept)
        for j in range(cols // 128):
            at = pl.ds(pl.multiple_of(col + j * 128, 128), 128)
            lanes = slice(j * 128, (j + 1) * 128)
            states = xs_ref[seq, SKIP:, lanes].astype(jnp.float32)[MIN_PROMPT - SKIP :]
            hidden = jnp.where(mask_ref[seq] > 0.0, embed_ref[:, at], states)
            own_ref[rows, lanes] = (hidden * gain_ref[:, at]).astype(jnp.bfloat16)

    multiply(units, blocks, mask_ref, gain_ref, embed_ref, acc_ref, sq_ref, (normed_a, normed_b), True)
    for copy in after:
        copy.wait()


def next_kernel(units, following, *refs):
    mask_ref, gain_ref, embed_ref, x_ref, w_ref, _, acc_in, sq_in, x_now, w_now, acc_ref, sq_ref = refs[:12]
    refs = refs[12:]
    after = []
    if following:
        x_next, w_next, normed_a, normed_b, sems = refs
        for i, unit in enumerate(following):
            after += fetch(x_ref, w_ref, unit, x_next, w_next, i, sems.at[i])
    else:
        normed_a, normed_b, sems = refs
    for copy in after:
        copy.start()
    blocks = [(x_now, w_now, i, []) for i in range(len(units))]
    multiply(units, blocks, mask_ref, gain_ref, embed_ref, acc_ref, sq_ref, (normed_a, normed_b), False)
    for copy in after:
        copy.wait()


VMEM = pl.BlockSpec(memory_space=pltpu.VMEM)
SMEM = pl.BlockSpec(memory_space=pltpu.SMEM)
HBM = pl.BlockSpec(memory_space=pltpu.HBM)
ANY = pl.BlockSpec(memory_space=pl.ANY)


def block_shapes(x, w, count):
    seqs, length, _ = x.shape
    return ((count, seqs, length - SKIP, UNIT), jnp.bfloat16), ((count, UNIT, w.shape[1]), jnp.bfloat16)


def cost(rows, cols, units):
    return pl.CostEstimate(
        flops=2 * rows * UNIT * len(units) * cols,
        bytes_accessed=2 * UNIT * len(units) * (rows + cols),
        transcendentals=0,
    )


def main_head(place, prompt_len, bits, gain, embed, x, w, token, units, following):
    seqs, length, _ = x.shape
    kept = length - MIN_PROMPT
    rows, cols = seqs * kept, w.shape[1]
    shapes = [
        ((rows, cols), jnp.float32),
        ((rows, 128), jnp.float32),
        ((seqs, kept, 128), jnp.float32),
        ((rows, cols), jnp.bfloat16),
        ((seqs, length, cols), jnp.bfloat16),
        *block_shapes(x, w, len(following)),
    ]
    return pl.pallas_call(
        functools.partial(head_kernel, units, following),
        in_specs=[SMEM, SMEM, VMEM, VMEM, VMEM, HBM, HBM, ANY],
        out_specs=[VMEM] * len(shapes),
        out_shape=[jax.ShapeDtypeStruct(*s) for s in shapes],
        scratch_shapes=[
            *[pltpu.VMEM(*s) for s in block_shapes(x, w, len(units))],
            pltpu.VMEM((rows, UNIT), jnp.bfloat16),
            pltpu.VMEM((rows, UNIT), jnp.bfloat16),
            pltpu.SemaphoreType.DMA((len(units) + len(following), 2)),
            pltpu.SemaphoreType.DMA,
        ],
        compiler_params=pltpu.CompilerParams(vmem_limit_bytes=36 * MIB),
        cost_estimate=cost(rows, cols, units),
        name="main_head",
    )(place, prompt_len, bits, gain, embed, x, w, token)


def main_next(mask, gain, embed, x, w, token, acc, sq, x_now, w_now, units, following):
    rows, cols = acc.shape
    shapes = [(acc.shape, jnp.float32), (sq.shape, jnp.float32)]
    if following:
        shapes += block_shapes(x, w, len(following))
    return pl.pallas_call(
        functools.partial(next_kernel, units, following),
        in_specs=[VMEM, VMEM, VMEM, HBM, HBM, ANY, VMEM, VMEM, VMEM, VMEM],
        out_specs=[VMEM] * len(shapes),
        out_shape=[jax.ShapeDtypeStruct(*s) for s in shapes],
        input_output_aliases={6: 0, 7: 1},
        scratch_shapes=[
            pltpu.VMEM((rows, UNIT), jnp.bfloat16),
            pltpu.VMEM((rows, UNIT), jnp.bfloat16),
            pltpu.SemaphoreType.DMA((max(len(following), 1), 2)),
        ],
        compiler_params=pltpu.CompilerParams(vmem_limit_bytes=20 * MIB),
        cost_estimate=cost(rows, cols, units),
        name="main_next",
    )(mask, gain, embed, x, w, token, acc, sq, x_now, w_now)


def low_rank_kernel(place_ref, own_ref, mine_ref, other_ref, out_ref):
    rows, cols = own_ref.shape
    half = out_ref.shape[0]
    width = cols // 2
    core = place_ref[1]
    dims = (((1,), (1,)), ((), ()))
    mine = own_ref[:, pl.ds(pl.multiple_of(core * width, width), width)]
    other = own_ref[:, pl.ds(pl.multiple_of((1 - core) * width, width), width)]
    prod = lax.dot_general(mine, mine_ref[...], dims, preferred_element_type=jnp.float32)
    prod += lax.dot_general(other, other_ref[...], dims, preferred_element_type=jnp.float32)
    rank = prod.shape[1]
    tail = jnp.concatenate([prod[half:], jnp.zeros((2 * half - rows, rank), jnp.float32)], axis=0)
    out_ref[...] = jnp.concatenate([prod[:half], tail], axis=1).astype(jnp.bfloat16)


def low_rank(place, own, mine, other):
    half = -(-own.shape[0] // 32) * 16
    return pl.pallas_call(
        low_rank_kernel,
        in_specs=[SMEM, VMEM, VMEM, VMEM],
        out_specs=VMEM,
        out_shape=jax.ShapeDtypeStruct((half, 2 * mine.shape[0]), jnp.bfloat16),
        compiler_params=pltpu.CompilerParams(vmem_limit_bytes=8 * MIB),
        name="low_rank",
    )(place, own, mine, other)


def final_kernel(
    place_ref, prompt_ref, embed_ref, mine_ref, r1_ref, r2_ref, r3_ref, a_ref, acc_ref, sq_ref, mask_ref, xs_ref,
    out_ref, stage_ref, sems,
):
    seqs, kept, _ = mask_ref.shape
    cols = acc_ref.shape[1]
    rank = a_ref.shape[0]
    half = mine_ref.shape[0]
    col = pl.multiple_of(place_ref[0], cols)
    embed = embed_ref[:, pl.ds(col, cols)]
    total = mine_ref[...].astype(jnp.float32) + r1_ref[...].astype(jnp.float32)
    total += r2_ref[...].astype(jnp.float32) + r3_ref[...].astype(jnp.float32)
    low = jnp.concatenate([total[:, :rank], total[: seqs * kept - half, rank:]], axis=0)
    copies = []
    for seq in range(seqs):
        rows = slice(seq * kept, (seq + 1) * kept)
        adapter = jnp.dot(low[rows].astype(jnp.bfloat16), a_ref[...], preferred_element_type=jnp.float32)
        mean = jnp.sum(sq_ref[rows], axis=1, keepdims=True) * (1.0 / FEATURES)
        scale = lax.rsqrt(mean + norm_epsilon)
        position = lax.broadcasted_iota(jnp.int32, (kept, 1), 0) + MIN_PROMPT
        response = position >= prompt_ref[seq]
        states = xs_ref[seq].astype(jnp.float32)
        head, states = states[:MIN_PROMPT], states[MIN_PROMPT:]
        hidden = jnp.where(mask_ref[seq][:, :1] > 0.0, embed, states)
        projected = (acc_ref[rows] + adapter_scale * adapter) * scale
        value = jnp.where(response, hidden + projected, states)
        stage_ref[seq] = jnp.concatenate([head, value], axis=0).astype(jnp.bfloat16)
        copy = pltpu.make_async_copy(stage_ref.at[seq], out_ref.at[seq], sems.at[seq])
        copy.start()
        copies.append(copy)
    for copy in copies:
        copy.wait()


def final(place, prompt_len, embed, mine, received, a, acc, sq, mask, xs):
    return pl.pallas_call(
        final_kernel,
        in_specs=[SMEM, SMEM] + [VMEM] * 10,
        out_specs=HBM,
        out_shape=jax.ShapeDtypeStruct(xs.shape, jnp.bfloat16),
        scratch_shapes=[pltpu.VMEM(xs.shape, jnp.bfloat16), pltpu.SemaphoreType.DMA((xs.shape[0],))],
        compiler_params=pltpu.CompilerParams(vmem_limit_bytes=20 * MIB),
        name="final",
    )(place, prompt_len, embed, mine, *received, a, acc, sq, mask, xs)


def local(x, mask_bits, prompt_len, weight, norm_gain, mask_embed, grads, factors, first_moment, second_moment):
    width = x.shape[2]
    cols = weight.shape[1]
    half = cols // 2
    core = lax.axis_index("c")
    col_start = lax.axis_index(TENSOR) * cols
    rank = factors.shape[1]
    share = rank // 16

    def own_half(v):
        return lax.dynamic_slice_in_dim(v, core * half, half, v.ndim - 1)

    def other_half(v):
        return lax.dynamic_slice_in_dim(v, (1 - core) * half, half, v.ndim - 1)

    grad = grads[0]
    from_core = exchange(bf16(other_half(grad)), "c", (1,))
    total = own_half(grad) + f32(from_core)
    sent = bf16(total)
    from_y = [exchange(sent, "y", (k,)) for k in (2, 3, 1)]
    total = total + f32(from_y[0]) + f32(from_y[1]) + f32(from_y[2])
    from_z = exchange(bf16(total), ("zh",), (1,))
    total = total + f32(from_z)

    new_first, new_second = adam_update(total, own_half(first_moment), own_half(second_moment))
    shipped = bf16(factor_update(new_first, new_second, own_half(factors)))
    b_own = shipped[1]
    b_other = exchange(b_own, "c", (1,))
    a_own = shipped[0]
    a_other = exchange(a_own, "c", (1,))

    my_row = lax.axis_index(DP) * share
    pair_row = (lax.axis_index(DP) + 1 - 2 * core) * share
    rows_out = lax.dynamic_slice_in_dim(total, pair_row, share, 1)
    rows_in = exchange(rows_out, "c", (1,))
    rows_mine = lax.dynamic_slice_in_dim(total, my_row, share, 1)

    def ordered(mine, others):
        return jnp.where(
            core == 0, jnp.concatenate([mine, others], -1), jnp.concatenate([others, mine], -1)
        )

    row_total = ordered(rows_mine, rows_in)
    out_first, out_second = adam_update(
        row_total,
        lax.dynamic_slice_in_dim(first_moment, my_row, share, 1),
        lax.dynamic_slice_in_dim(second_moment, my_row, share, 1),
    )

    gain = norm_gain.reshape(1, width)
    embed = f32(mask_embed).reshape(1, width)
    place = jnp.stack([col_start, core]).astype(jnp.int32)
    parts = [(0, 1, 2, 3), (4, 5), (6,), (7,)]
    acc, sq, mask, own_normed, xs, x_next, w_next = main_head(
        place, prompt_len, mask_bits, gain, embed, x, weight, from_core, parts[0], parts[1]
    )
    acc, sq, x_next, w_next = main_next(
        mask, gain, embed, x, weight, from_y[0], acc, sq, x_next, w_next, parts[1], parts[2]
    )
    low = low_rank(place, own_normed, b_own, b_other)
    from_zl = exchange(low, ("zl",), (1,))
    acc, sq, x_next, w_next = main_next(
        mask, gain, embed, x, weight, b_other, acc, sq, x_next, w_next, parts[2], parts[3]
    )
    low = bf16(f32(low) + f32(from_zl))
    from_x = [exchange(low, ("x",), (k,)) for k in (2, 3, 1)]
    acc, sq = main_next(mask, gain, embed, x, weight, from_zl, acc, sq, x_next, w_next, parts[3], ())
    a_full = ordered(a_own, a_other)
    out = final(place, prompt_len, embed, low, from_x, a_full, acc, sq, mask, xs)
    return out, out_first, out_second


def solution(mesh):
    split = Mesh(mesh.devices.reshape(2, 4, 2, 4, 2), ("zh", "y", "c", "x", "zl"))
    placed = (
        P(DP, None, None),
        P(DP, None),
        P(DP),
        P(None, TENSOR),
        P(),
        P(),
        P(DP, None, None, TENSOR),
        P(None, None, TENSOR),
        P(None, None, TENSOR),
        P(None, None, TENSOR),
    )
    return jax.shard_map(
        local,
        mesh=split,
        in_specs=placed,
        out_specs=(P(DP, None, TENSOR), P(None, DP, TENSOR), P(None, DP, TENSOR)),
        check_vma=False,
    )
```

```python
import functools
import itertools

import jax
import jax.numpy as jnp
from jax import lax
from jax.experimental import pallas as pl
from jax.experimental.pallas import tpu as pltpu
from jax.sharding import Mesh, PartitionSpec as P

beta_one = 0.9
beta_two = 0.999
learn_rate = 0.03
adam_count = 100
epsilon = 1e-08
adapter_scale = 2.0
norm_epsilon = 1e-05

SIZES = {"zh": 2, "y": 4, "c": 2, "x": 4, "zl": 2}
DP = ("zh", "y", "c")
TENSOR = ("x", "zl")
UNIT = 1024
FEATURES = 8192
MIN_PROMPT = 24
SKIP = 16
MIB = 1 << 20


def f32(v):
    return v.astype(jnp.float32)


def bf16(v):
    return v.astype(jnp.bfloat16)


def exchange(v, axes, key):
    ids = list(itertools.product(*[range(SIZES[a]) for a in axes]))
    index = {t: i for i, t in enumerate(ids)}
    pairs = [(index[t], index[tuple(a ^ k for a, k in zip(t, key))]) for t in ids]
    return lax.ppermute(v, tuple(axes), pairs)


def adam_update(summed_grad, first_moment, second_moment):
    new_first = beta_one * first_moment + (1.0 - beta_one) * summed_grad
    new_second = beta_two * second_moment + (1.0 - beta_two) * summed_grad * summed_grad
    return new_first, new_second


def factor_update(new_first, new_second, param_rows):
    step_size = learn_rate / (1.0 - beta_one**adam_count)
    divisor = jnp.sqrt(new_second / (1.0 - beta_two**adam_count)) + epsilon
    return param_rows - step_size * new_first / divisor


def hidden_block(x_ref, mask_ref, embed, seq, lanes):
    states = x_ref[seq, :, lanes].astype(jnp.float32)[MIN_PROMPT - SKIP :]
    return jnp.where(mask_ref[seq] > 1.5, embed, states)


def normalise(x_ref, mask_ref, gain_ref, embed_ref, k0, normed_ref, sq_ref, first):
    seqs, kept, _ = mask_ref.shape
    for seq in range(seqs):
        rows = slice(seq * kept, (seq + 1) * kept)
        squares = None if first else sq_ref[rows]
        for j in range(UNIT // 128):
            at = slice(k0 + j * 128, k0 + (j + 1) * 128)
            lanes = slice(j * 128, (j + 1) * 128)
            hidden = hidden_block(x_ref, mask_ref, embed_ref[:, at], seq, lanes)
            squares = hidden * hidden if squares is None else squares + hidden * hidden
            normed_ref[rows, lanes] = (hidden * gain_ref[:, at]).astype(jnp.bfloat16)
        sq_ref[rows] = squares


def fetch(x_ref, w_ref, unit, x_dst, w_dst, sem):
    k0 = unit * UNIT
    return [
        pltpu.make_async_copy(w_ref.at[pl.ds(k0, UNIT)], w_dst, sem.at[0]),
        pltpu.make_async_copy(x_ref.at[:, pl.ds(SKIP, x_ref.shape[1] - SKIP), pl.ds(k0, UNIT)], x_dst, sem.at[1]),
    ]


def start(copies):
    for copy in copies:
        copy.start()


def wait(copies):
    for copy in copies:
        copy.wait()


def multiply(blocks, mask_ref, gain_ref, embed_ref, acc_ref, sq_ref, normed, fresh):
    def ready(i):
        unit, x_buf, _, copies = blocks[i]
        wait(copies)
        normalise(x_buf, mask_ref, gain_ref, embed_ref, unit * UNIT, normed[i % 2], sq_ref, fresh and i == 0)

    ready(0)
    for i in range(len(blocks)):
        if i + 1 < len(blocks):
            ready(i + 1)
        product = jnp.dot(normed[i % 2][...], blocks[i][2][...], preferred_element_type=jnp.float32)
        if fresh and i == 0:
            acc_ref[...] = product
        else:
            acc_ref[...] += product


def pack_kernel(grad_ref, own_ref, other_ref, wide_ref, sems):
    width = own_ref.shape[2]
    core = lax.axis_index("c")
    near = pl.ds(pl.multiple_of(core * width, width), width)
    far = pl.ds(pl.multiple_of((1 - core) * width, width), width)
    other = pltpu.make_async_copy(grad_ref.at[0, :, :, far], wide_ref, sems.at[0])
    own = pltpu.make_async_copy(grad_ref.at[0, :, :, near], own_ref, sems.at[1])
    other.start()
    own.start()
    other.wait()
    other_ref[...] = wide_ref[...].astype(jnp.bfloat16)
    own.wait()


def pack(grads):
    _, two, rank, cols = grads.shape
    shape = (two, rank, cols // 2)
    return pl.pallas_call(
        pack_kernel,
        in_specs=[HBM],
        out_specs=[VMEM, VMEM],
        out_shape=[jax.ShapeDtypeStruct(shape, jnp.float32), jax.ShapeDtypeStruct(shape, jnp.bfloat16)],
        scratch_shapes=[pltpu.VMEM(shape, jnp.float32), pltpu.SemaphoreType.DMA((2,))],
        compiler_params=pltpu.CompilerParams(vmem_limit_bytes=8 * MIB),
        name="pack",
    )(in_hbm(grads))


def head_kernel(units, following, *refs):
    prompt_ref, bits_ref, gain_ref, embed_ref, x_ref, w_ref, _ = refs[:7]
    acc_ref, sq_ref, mask_ref, mine_ref, other_ref, xs_ref, gain_out = refs[7:14]
    ahead = refs[14 : 14 + 2 * len(following)]
    refs = refs[14 + 2 * len(following) :]
    bufs = refs[: 2 * len(units)]
    normed_a, normed_b, prompt_buf, bits_buf, sems, own_sems = refs[2 * len(units) :]
    seqs, kept, _ = mask_ref.shape
    cols = xs_ref.shape[2]
    width = cols // 2
    col = pl.multiple_of((lax.axis_index("x") * 2 + lax.axis_index("zl")) * cols, cols)
    core = lax.axis_index("c")
    small = [
        pltpu.make_async_copy(prompt_ref, prompt_buf, own_sems.at[0]),
        pltpu.make_async_copy(bits_ref, bits_buf, own_sems.at[1]),
        pltpu.make_async_copy(gain_ref, gain_out, own_sems.at[2]),
    ]
    start(small)
    own = pltpu.make_async_copy(x_ref.at[:, :, pl.ds(col, cols)], xs_ref, own_sems.at[3])
    own.start()
    blocks = []
    for i, unit in enumerate(units):
        copies = fetch(x_ref, w_ref, unit, bufs[2 * i], bufs[2 * i + 1], sems.at[i])
        start(copies)
        blocks.append((unit, bufs[2 * i], bufs[2 * i + 1], copies))
    after = []
    for i, unit in enumerate(following):
        after += fetch(x_ref, w_ref, unit, ahead[2 * i], ahead[2 * i + 1], sems.at[len(units) + i])
    start(after)

    wait(small)
    length = bits_buf.shape[1]
    here = lax.broadcasted_iota(jnp.int32, (kept, length), 0) + MIN_PROMPT
    there = lax.broadcasted_iota(jnp.int32, (kept, length), 1)
    position = lax.broadcasted_iota(jnp.int32, (kept, 1), 0) + MIN_PROMPT
    for seq in range(seqs):
        bits = jnp.where(here == there, bits_buf[seq : seq + 1, :], 0)
        chosen = 1.0 + jnp.sum((bits == 1).astype(jnp.float32), axis=1, keepdims=True)
        column = jnp.where(position >= prompt_buf[0:1, seq : seq + 1], chosen, 0.0)
        mask_ref[seq] = jnp.broadcast_to(column, (kept, 128))

    own.wait()
    for at_core, dst in ((core, mine_ref), (1 - core, other_ref)):
        for seq in range(seqs):
            rows = slice(seq * kept, (seq + 1) * kept)
            for j in range(width // 128):
                lanes = pl.multiple_of(at_core * width + j * 128, 128)
                states = xs_ref[seq, SKIP:, pl.ds(lanes, 128)].astype(jnp.float32)[MIN_PROMPT - SKIP :]
                at = pl.ds(pl.multiple_of(col + lanes, 128), 128)
                hidden = jnp.where(mask_ref[seq] > 1.5, embed_ref[:, at], states)
                dst[rows, j * 128 : (j + 1) * 128] = (hidden * gain_out[:, at]).astype(jnp.bfloat16)

    multiply(blocks, mask_ref, gain_out, embed_ref, acc_ref, sq_ref, (normed_a, normed_b), True)
    wait(after)


def half_copies(sources, targets, core, sems):
    width = targets[0].shape[2]
    at = pl.ds(pl.multiple_of(core * width, width), width)
    return [pltpu.make_async_copy(s.at[:, :, at], t, sems.at[i]) for i, (s, t) in enumerate(zip(sources, targets))]


def next_kernel(units, following, factors, *refs):
    mask_ref, gain_ref, embed_ref, x_ref, w_ref, _, acc_in, sq_in = refs[:8]
    now = refs[8 : 8 + 2 * len(units)]
    refs = refs[8 + 2 * len(units) :]
    if factors:
        params, refs = refs[:3], refs[3:]
    acc_ref, sq_ref = refs[:2]
    ahead = refs[2 : 2 + 2 * len(following)]
    refs = refs[2 + 2 * len(following) :]
    if factors:
        halves, eights, refs = refs[:3], refs[3:5], refs[5:]
    normed_a, normed_b, sems = refs[:3]
    after = []
    if factors:
        after += half_copies(params, halves, lax.axis_index("c"), refs[3])
        at = pl.ds(pl.multiple_of((lax.axis_index("zh") * 4 + lax.axis_index("y")) * 8, 8), 8)
        for i in range(2):
            after.append(pltpu.make_async_copy(params[1 + i].at[:, at], eights[i], refs[3].at[3 + i]))
    for i, unit in enumerate(following):
        after += fetch(x_ref, w_ref, unit, ahead[2 * i], ahead[2 * i + 1], sems.at[i])
    start(after)
    blocks = [(unit, now[2 * i], now[2 * i + 1], []) for i, unit in enumerate(units)]
    multiply(blocks, mask_ref, gain_ref, embed_ref, acc_ref, sq_ref, (normed_a, normed_b), False)
    wait(after)


def last_kernel(units, *refs):
    mask_ref, gain_ref, embed_ref, _, acc_in, sq_in, xs_ref, a_mine, a_other = refs[:9]
    rows_mine, rows_other, first_ref, second_ref = refs[9:13]
    now = refs[13 : 13 + 2 * len(units)]
    acc_ref, sq_ref, base_ref, scale_ref, a_ref, first_out, second_out = refs[13 + 2 * len(units) :][:7]
    normed_a, normed_b, first_buf, second_buf, sems = refs[20 + 2 * len(units) :]
    seqs, kept, _ = mask_ref.shape
    cols = xs_ref.shape[2]
    width = cols // 2
    col = pl.multiple_of((lax.axis_index("x") * 2 + lax.axis_index("zl")) * cols, cols)
    even = lax.axis_index("c") == 0

    a_ref[:, :width] = jnp.where(even, a_mine[...], a_other[...])
    a_ref[:, width:] = jnp.where(even, a_other[...], a_mine[...])
    mine, other = rows_mine[...], rows_other[...]
    summed = jnp.concatenate([jnp.where(even, mine, other), jnp.where(even, other, mine)], axis=2)
    share = summed.shape[1] // 2
    first, second = adam_update(summed, first_ref[...], second_ref[...])
    first_buf[...] = jnp.where(even, first[:, :share], first[:, share:])
    second_buf[...] = jnp.where(even, second[:, :share], second[:, share:])
    out = [
        pltpu.make_async_copy(first_buf, first_out, sems.at[0]),
        pltpu.make_async_copy(second_buf, second_out, sems.at[1]),
    ]
    start(out)

    blocks = [(unit, now[2 * i], now[2 * i + 1], []) for i, unit in enumerate(units)]
    multiply(blocks, mask_ref, gain_ref, embed_ref, acc_ref, sq_ref, (normed_a, normed_b), False)
    for seq in range(seqs):
        rows = slice(seq * kept, (seq + 1) * kept)
        mean = jnp.sum(sq_ref[rows], axis=1, keepdims=True) * (1.0 / FEATURES)
        scale = jnp.broadcast_to(lax.rsqrt(mean + norm_epsilon), (kept, 128))
        code = mask_ref[seq]
        scale_ref[rows] = jnp.where(code > 0.5, adapter_scale * scale, 0.0)
        for j in range(cols // 128):
            lanes = slice(j * 128, (j + 1) * 128)
            at = pl.ds(pl.multiple_of(col + j * 128, 128), 128)
            states = xs_ref[seq, :, lanes].astype(jnp.float32)
            head, states = states[:MIN_PROMPT], states[MIN_PROMPT:]
            hidden = jnp.where(code > 1.5, embed_ref[:, at], states)
            value = jnp.where(code > 0.5, hidden + scale * acc_ref[rows, lanes], states)
            base_ref[seq, :MIN_PROMPT, lanes] = head
            base_ref[seq, MIN_PROMPT:, lanes] = value
    wait(out)


VMEM = pl.BlockSpec(memory_space=pltpu.VMEM)
SMEM = pl.BlockSpec(memory_space=pltpu.SMEM)
HBM = pl.BlockSpec(memory_space=pltpu.HBM)
ANY = pl.BlockSpec(memory_space=pl.ANY)


def in_hbm(v):
    return pltpu.with_memory_space_constraint(v, pltpu.HBM)


def block_shapes(x, w, count):
    seqs, length, _ = x.shape
    return [((seqs, length - SKIP, UNIT), jnp.bfloat16), ((UNIT, w.shape[1]), jnp.bfloat16)] * count


def cost(rows, cols, units):
    return pl.CostEstimate(
        flops=2 * rows * UNIT * len(units) * cols,
        bytes_accessed=2 * UNIT * len(units) * (rows + cols),
        transcendentals=0,
    )


def small_call(kernel, shapes, name, *args):
    in_specs = [ANY if isinstance(v, tuple) else VMEM for v in args]
    args = [v[0] if isinstance(v, tuple) else v for v in args]
    return pl.pallas_call(
        kernel,
        in_specs=in_specs,
        out_specs=[VMEM] * len(shapes),
        out_shape=[jax.ShapeDtypeStruct(*v) for v in shapes],
        compiler_params=pltpu.CompilerParams(vmem_limit_bytes=4 * MIB),
        name=name,
    )(*args)


def main_head(prompt_len, bits, gain, embed, x, w, token, units, following):
    seqs, length, width = x.shape
    kept = length - MIN_PROMPT
    rows, cols = seqs * kept, w.shape[1]
    shapes = [
        ((rows, cols), jnp.float32),
        ((rows, 128), jnp.float32),
        ((seqs, kept, 128), jnp.float32),
        ((rows, cols // 2), jnp.bfloat16),
        ((rows, cols // 2), jnp.bfloat16),
        ((seqs, length, cols), jnp.bfloat16),
        ((1, width), jnp.float32),
        *block_shapes(x, w, len(following)),
    ]
    out = pl.pallas_call(
        functools.partial(head_kernel, units, following),
        in_specs=[HBM, HBM, HBM, VMEM, HBM, HBM, ANY],
        out_specs=[VMEM] * len(shapes),
        out_shape=[jax.ShapeDtypeStruct(*s) for s in shapes],
        scratch_shapes=[
            *[pltpu.VMEM(*s) for s in block_shapes(x, w, len(units))],
            pltpu.VMEM((rows, UNIT), jnp.bfloat16),
            pltpu.VMEM((rows, UNIT), jnp.bfloat16),
            pltpu.VMEM(prompt_len.shape, jnp.int32),
            pltpu.VMEM(bits.shape, jnp.int32),
            pltpu.SemaphoreType.DMA((len(units) + len(following), 2)),
            pltpu.SemaphoreType.DMA((4,)),
        ],
        compiler_params=pltpu.CompilerParams(vmem_limit_bytes=20 * MIB),
        cost_estimate=cost(rows, cols, units),
        name="main_head",
    )(in_hbm(prompt_len), in_hbm(bits), in_hbm(gain), embed, in_hbm(x), in_hbm(w), token)
    return out[:7], out[7:]


def main_next(mask, gain, embed, x, w, token, acc, sq, now, units, following, params=()):
    rows, cols = acc.shape
    shapes = [(acc.shape, jnp.float32), (sq.shape, jnp.float32), *block_shapes(x, w, len(following))]
    if params:
        two, rank, _ = params[0].shape
        shapes += [((two, rank, cols // 2), jnp.float32)] * 3 + [((two, 8, cols), jnp.float32)] * 2
    out = pl.pallas_call(
        functools.partial(next_kernel, units, following, bool(params)),
        in_specs=[VMEM, VMEM, VMEM, HBM, HBM, ANY, VMEM, VMEM] + [VMEM] * len(now) + [HBM] * len(params),
        out_specs=[VMEM] * len(shapes),
        out_shape=[jax.ShapeDtypeStruct(*s) for s in shapes],
        input_output_aliases={6: 0, 7: 1},
        scratch_shapes=[
            pltpu.VMEM((rows, UNIT), jnp.bfloat16),
            pltpu.VMEM((rows, UNIT), jnp.bfloat16),
            pltpu.SemaphoreType.DMA((len(following), 2)),
            *([pltpu.SemaphoreType.DMA((5,))] if params else []),
        ],
        compiler_params=pltpu.CompilerParams(vmem_limit_bytes=12 * MIB),
        cost_estimate=cost(rows, cols, units),
        name="main_next",
    )(mask, gain, embed, in_hbm(x), in_hbm(w), token, acc, sq, *now, *[in_hbm(v) for v in params])
    ahead = 2 + 2 * len(following)
    return out[:2], out[2:ahead], out[ahead:]


def main_last(mask, gain, embed, token, acc, sq, xs, a_mine, a_other, moments, now, units):
    rows, cols = acc.shape
    rank = a_mine.shape[0]
    out_rows = (2, 4, cols)
    shapes = [
        (acc.shape, jnp.float32),
        (sq.shape, jnp.float32),
        (xs.shape, jnp.float32),
        (sq.shape, jnp.float32),
        ((rank, cols), jnp.bfloat16),
        (out_rows, jnp.float32),
        (out_rows, jnp.float32),
    ]
    return pl.pallas_call(
        functools.partial(last_kernel, units),
        in_specs=[VMEM, VMEM, VMEM, ANY] + [VMEM] * (9 + len(now)),
        out_specs=[VMEM] * 5 + [HBM] * 2,
        out_shape=[jax.ShapeDtypeStruct(*s) for s in shapes],
        input_output_aliases={4: 0, 5: 1},
        scratch_shapes=[
            pltpu.VMEM((rows, UNIT), jnp.bfloat16),
            pltpu.VMEM((rows, UNIT), jnp.bfloat16),
            pltpu.VMEM(out_rows, jnp.float32),
            pltpu.VMEM(out_rows, jnp.float32),
            pltpu.SemaphoreType.DMA((2,)),
        ],
        compiler_params=pltpu.CompilerParams(vmem_limit_bytes=12 * MIB),
        cost_estimate=cost(rows, cols, units),
        name="main_last",
    )(mask, gain, embed, token, acc, sq, xs, a_mine, a_other, *moments, *now)[2:]


def add_kernel(mine_ref, theirs_ref, *refs):
    refs[-1][...] = (mine_ref[...].astype(jnp.float32) + theirs_ref[...].astype(jnp.float32)).astype(jnp.bfloat16)


def gather_sum_kernel(mine_ref, r1_ref, r2_ref, r3_ref, _, total_ref, sent_ref):
    total = mine_ref[...] + r1_ref[...].astype(jnp.float32)
    total += r2_ref[...].astype(jnp.float32) + r3_ref[...].astype(jnp.float32)
    total_ref[...] = total
    sent_ref[...] = total.astype(jnp.bfloat16)


def update_kernel(total_ref, theirs_ref, factors_ref, first_ref, second_ref, _, a_ref, b_ref, rows_ref, sum_ref):
    total = total_ref[...] + theirs_ref[...].astype(jnp.float32)
    new_first, new_second = adam_update(total, first_ref[...], second_ref[...])
    shipped = factor_update(new_first, new_second, factors_ref[...]).astype(jnp.bfloat16)
    a_ref[...] = shipped[0]
    b_ref[...] = shipped[1]
    at = pl.ds(pl.multiple_of((lax.axis_index("zh") * 4 + lax.axis_index("y")) * 8, 8), 8)
    sum_ref[...] = total
    rows_ref[...] = sum_ref[:, at]


def low_rank_kernel(own_mine_ref, own_other_ref, mine_ref, other_ref, out_ref):
    rows = own_mine_ref.shape[0]
    half = out_ref.shape[0]
    dims = (((1,), (1,)), ((), ()))
    prod = lax.dot_general(own_mine_ref[...], mine_ref[...], dims, preferred_element_type=jnp.float32)
    prod += lax.dot_general(own_other_ref[...], other_ref[...], dims, preferred_element_type=jnp.float32)
    rank = prod.shape[1]
    tail = jnp.concatenate([prod[half:], jnp.zeros((2 * half - rows, rank), jnp.float32)], axis=0)
    out_ref[...] = jnp.concatenate([prod[:half], tail], axis=1).astype(jnp.bfloat16)


def low_rank(own_mine, own_other, mine, other):
    half = -(-own_mine.shape[0] // 32) * 16
    return pl.pallas_call(
        low_rank_kernel,
        in_specs=[VMEM] * 4,
        out_specs=VMEM,
        out_shape=jax.ShapeDtypeStruct((half, 2 * mine.shape[0]), jnp.bfloat16),
        compiler_params=pltpu.CompilerParams(vmem_limit_bytes=8 * MIB),
        name="low_rank",
    )(own_mine, own_other, mine, other)


def final_kernel(mine_ref, r1_ref, r2_ref, r3_ref, a_ref, base_ref, scale_ref, out_ref, stage_ref, sems):
    seqs, length, _ = base_ref.shape
    kept = length - MIN_PROMPT
    rank = a_ref.shape[0]
    half = mine_ref.shape[0]
    total = mine_ref[...].astype(jnp.float32) + r1_ref[...].astype(jnp.float32)
    total += r2_ref[...].astype(jnp.float32) + r3_ref[...].astype(jnp.float32)
    low = jnp.concatenate([total[:, :rank], total[: seqs * kept - half, rank:]], axis=0)
    low = low * scale_ref[:, :rank]
    copies = []
    for seq in range(seqs):
        rows = slice(seq * kept, (seq + 1) * kept)
        adapter = jnp.dot(low[rows].astype(jnp.bfloat16), a_ref[...], preferred_element_type=jnp.float32)
        value = jnp.concatenate([base_ref[seq, :MIN_PROMPT], base_ref[seq, MIN_PROMPT:] + adapter], axis=0)
        stage_ref[seq] = value.astype(jnp.bfloat16)
        copy = pltpu.make_async_copy(stage_ref.at[seq], out_ref.at[seq], sems.at[seq])
        copy.start()
        copies.append(copy)
    for copy in copies:
        copy.wait()


def final(mine, received, a, base, scale):
    return pl.pallas_call(
        final_kernel,
        in_specs=[VMEM] * 7,
        out_specs=HBM,
        out_shape=jax.ShapeDtypeStruct(base.shape, jnp.bfloat16),
        scratch_shapes=[pltpu.VMEM(base.shape, jnp.bfloat16), pltpu.SemaphoreType.DMA((base.shape[0],))],
        compiler_params=pltpu.CompilerParams(vmem_limit_bytes=20 * MIB),
        name="final",
    )(mine, *received, a, base, scale)


def local(x, mask_bits, prompt_len, weight, norm_gain, mask_embed, grads, factors, first_moment, second_moment):
    width = x.shape[2]
    cols = weight.shape[1]
    rank = factors.shape[1]
    wide, narrow = jnp.float32, jnp.bfloat16

    gain = norm_gain.reshape(1, width)
    embed = f32(mask_embed).reshape(1, width)

    total, outgoing = pack(grads)
    from_core = exchange(outgoing, "c", (1,))
    total = total + f32(from_core)
    sent = bf16(total)
    from_y = [exchange(sent, "y", (k,)) for k in (1, 2, 3)]
    (acc, sq, mask, own_mine, own_other, xs, gain), at_z = main_head(
        prompt_len.reshape(1, -1), mask_bits, gain, embed, x, weight, from_core, (0, 1), (2, 3)
    )
    half = total.shape
    total, sent = small_call(gather_sum_kernel, [(half, wide), (half, narrow)], "sum_y", total, *from_y, (sq,))
    from_z = exchange(sent, ("zh",), (1,))
    (acc, sq), ahead, params = main_next(
        mask, gain, embed, x, weight, from_y[0], acc, sq, at_z, (2, 3), (4, 5),
        (factors, first_moment, second_moment),
    )

    a_own, b_own, rows_own, _ = small_call(
        update_kernel,
        [((rank, cols // 2), narrow), ((rank, cols // 2), narrow), ((2, 8, cols // 2), wide), (half, wide)],
        "update", total, from_z, *params[:3], (sq,),
    )
    b_other = exchange(b_own, "c", (1,))
    low = low_rank(own_mine, own_other, b_own, b_other)
    from_zl = exchange(low, ("zl",), (1,))
    (acc, sq), more, _ = main_next(mask, gain, embed, x, weight, b_other, acc, sq, ahead[:2], (4,), (6, 7))
    a_own, rows_own, _ = lax.optimization_barrier((a_own, rows_own, low))
    a_other = exchange(a_own, "c", (1,))
    rows_other = exchange(rows_own, "c", (1,))
    (low,) = small_call(add_kernel, [(low.shape, narrow)], "sum_zl", low, from_zl, (sq,))
    from_x = [exchange(low, ("x",), (k,)) for k in (1, 2, 3)]
    base, scale, a_full, out_first, out_second = main_last(
        mask, gain, embed, from_zl, acc, sq, xs, a_own, a_other, (rows_own, rows_other, *params[3:]),
        (*ahead[2:], *more), (5, 6, 7),
    )
    out = final(low, from_x, a_full, base, scale)
    return out, out_first, out_second


def solution(mesh):
    split = Mesh(mesh.devices.reshape(2, 4, 2, 4, 2), ("zh", "y", "c", "x", "zl"))
    placed = (
        P(DP, None, None),
        P(DP, None),
        P(DP),
        P(None, TENSOR),
        P(),
        P(),
        P(DP, None, None, TENSOR),
        P(None, None, TENSOR),
        P(None, None, TENSOR),
        P(None, None, TENSOR),
    )
    return jax.shard_map(
        local,
        mesh=split,
        in_specs=placed,
        out_specs=(P(DP, None, TENSOR), P(None, DP, TENSOR), P(None, DP, TENSOR)),
        check_vma=False,
    )
```

```python
import functools
import itertools

import jax
import jax.numpy as jnp
from jax import lax
from jax.experimental import pallas as pl
from jax.experimental.pallas import tpu as pltpu
from jax.sharding import Mesh, PartitionSpec as P

beta_one = 0.9
beta_two = 0.999
learn_rate = 0.03
adam_count = 100
epsilon = 1e-08
adapter_scale = 2.0
norm_epsilon = 1e-05

SIZES = {"zh": 2, "y": 4, "c": 2, "x": 4, "zl": 2}
DP = ("zh", "y", "c")
TENSOR = ("x", "zl")
CUTS = ((0, 1024, 2048, 3072), (3072, 4096, 5120), (5120, 6144), (6144, 7168, 8192))
FEATURES = 8192
MIN_PROMPT = 24
SKIP = 16
PIECE = 96
MIB = 1 << 20


def f32(v):
    return v.astype(jnp.float32)


def bf16(v):
    return v.astype(jnp.bfloat16)


def exchange(v, axes, key):
    ids = list(itertools.product(*[range(SIZES[a]) for a in axes]))
    index = {t: i for i, t in enumerate(ids)}
    pairs = [(index[t], index[tuple(a ^ k for a, k in zip(t, key))]) for t in ids]
    return lax.ppermute(v, tuple(axes), pairs)


def adam_update(summed_grad, first_moment, second_moment):
    new_first = beta_one * first_moment + (1.0 - beta_one) * summed_grad
    new_second = beta_two * second_moment + (1.0 - beta_two) * summed_grad * summed_grad
    return new_first, new_second


def factor_update(new_first, new_second, param_rows):
    step_size = learn_rate / (1.0 - beta_one**adam_count)
    divisor = jnp.sqrt(new_second / (1.0 - beta_two**adam_count)) + epsilon
    return param_rows - step_size * new_first / divisor


def normalise(x_ref, mask_ref, gain_ref, embed_ref, k0, normed_ref, sq_ref, first):
    seqs, kept, _ = mask_ref.shape
    for seq in range(seqs):
        rows = slice(seq * kept, (seq + 1) * kept)
        squares = None if first else sq_ref[rows]
        for j in range(normed_ref.shape[1] // 128):
            block = k0 // 128 + j
            states = x_ref[seq, SKIP:, k0 + j * 128 : k0 + (j + 1) * 128].astype(jnp.float32)[MIN_PROMPT - SKIP :]
            hidden = jnp.where(mask_ref[seq] > 1.5, embed_ref[block : block + 1], states)
            squares = hidden * hidden if squares is None else squares + hidden * hidden
            normed_ref[rows, j * 128 : (j + 1) * 128] = (hidden * gain_ref[block : block + 1]).astype(jnp.bfloat16)
        sq_ref[rows] = squares


def multiply(cuts, x_ref, w_ref, mask_ref, gain_ref, embed_ref, acc_ref, sq_ref, normed, begun=None):
    def block(i):
        if i == 0 and begun is not None:
            return begun
        return normed[i % 2].at[:, : cuts[i + 1] - cuts[i]]

    def ready(i):
        normalise(x_ref, mask_ref, gain_ref, embed_ref, cuts[i], block(i), sq_ref, False)

    count = len(cuts) - 1
    if begun is None:
        ready(0)
    for i in range(count):
        if i + 1 < count:
            ready(i + 1)
        product = jnp.dot(block(i)[...], w_ref[cuts[i] : cuts[i + 1]], preferred_element_type=jnp.float32)
        if i == 0 and begun is not None:
            acc_ref[...] = product
        else:
            acc_ref[...] += product


def start(copies):
    for copy in copies:
        copy.start()


def wait(copies):
    for copy in copies:
        copy.wait()


def tensor_index():
    return lax.axis_index("x") * 2 + lax.axis_index("zl")


def pack_kernel(grad_ref, own_ref, other_ref, wide_ref, sems):
    width = own_ref.shape[2]
    core = lax.axis_index("c")
    near = pl.ds(pl.multiple_of(core * width, width), width)
    far = pl.ds(pl.multiple_of((1 - core) * width, width), width)
    other = pltpu.make_async_copy(grad_ref.at[0, :, :, far], wide_ref, sems.at[0])
    own = pltpu.make_async_copy(grad_ref.at[0, :, :, near], own_ref, sems.at[1])
    other.start()
    own.start()
    other.wait()
    other_ref[...] = wide_ref[...].astype(jnp.bfloat16)
    own.wait()


def pack(grads):
    _, two, rank, cols = grads.shape
    shape = (two, rank, cols // 2)
    return pl.pallas_call(
        pack_kernel,
        in_specs=[HBM],
        out_specs=[VMEM, VMEM],
        out_shape=[jax.ShapeDtypeStruct(shape, jnp.float32), jax.ShapeDtypeStruct(shape, jnp.bfloat16)],
        scratch_shapes=[pltpu.VMEM(shape, jnp.float32), pltpu.SemaphoreType.DMA((2,))],
        compiler_params=pltpu.CompilerParams(vmem_limit_bytes=8 * MIB),
        cost_estimate=pl.CostEstimate(flops=20_000_000_000, bytes_accessed=80_000_000, transcendentals=0),
        name="pack",
    )(in_hbm(grads))


def prepare_kernel(
    first_block, prompt_ref, bits_ref, gain_ref, embed_ref, x_ref, _, mask_ref, mine_ref, other_ref, embed_out, sq_ref,
    normed_ref,
):
    seqs, kept, _ = mask_ref.shape
    width = mine_ref.shape[1]
    col = pl.multiple_of(tensor_index() * 2 * width, 2 * width)
    core = lax.axis_index("c")
    embed_out[...] = embed_ref[...].astype(jnp.float32)
    length = bits_ref.shape[1]
    here = lax.broadcasted_iota(jnp.int32, (kept, length), 0) + MIN_PROMPT
    there = lax.broadcasted_iota(jnp.int32, (kept, length), 1)
    position = lax.broadcasted_iota(jnp.int32, (kept, 1), 0) + MIN_PROMPT
    for seq in range(seqs):
        bits = jnp.where(here == there, bits_ref[seq : seq + 1, :], 0)
        chosen = 1.0 + jnp.sum((bits == 1).astype(jnp.float32), axis=1, keepdims=True)
        column = jnp.where(position >= prompt_ref[0:1, seq : seq + 1], chosen, 0.0)
        mask_ref[seq] = jnp.broadcast_to(column, (kept, 128))

    for at_core, dst in ((core, mine_ref), (1 - core, other_ref)):
        for seq in range(seqs):
            rows = slice(seq * kept, (seq + 1) * kept)
            for j in range(width // 128):
                lanes = pl.multiple_of(col + at_core * width + j * 128, 128)
                block = pl.ds(lanes // 128, 1)
                states = x_ref[seq, SKIP:, pl.ds(lanes, 128)].astype(jnp.float32)[MIN_PROMPT - SKIP :]
                hidden = jnp.where(mask_ref[seq] > 1.5, embed_out[block], states)
                dst[rows, j * 128 : (j + 1) * 128] = (hidden * gain_ref[block]).astype(jnp.bfloat16)
    normalise(x_ref, mask_ref, gain_ref, embed_out, first_block, normed_ref, sq_ref, True)


def y_kernel(
    cuts, normed_in, mask_ref, gain_ref, embed_ref, x_ref, w_ref, _, sq_in, acc_ref, sq_ref, normed_a, normed_b
):
    multiply(cuts, x_ref, w_ref, mask_ref, gain_ref, embed_ref, acc_ref, sq_ref, (normed_a, normed_b), normed_in)


def chip_rows():
    return pl.ds(pl.multiple_of((lax.axis_index("zh") * 4 + lax.axis_index("y")) * 8, 8), 8)


def core_lanes(width):
    return pl.ds(pl.multiple_of(lax.axis_index("c") * width, width), width)


def part_kernel(
    cuts, mask_ref, gain_ref, embed_ref, x_ref, w_ref, _, acc_in, sq_in, acc_ref, sq_ref, normed_a, normed_b
):
    multiply(cuts, x_ref, w_ref, mask_ref, gain_ref, embed_ref, acc_ref, sq_ref, (normed_a, normed_b))


def last_kernel(
    cuts, mask_ref, gain_ref, embed_ref, x_ref, w_ref, _, acc_in, sq_in, rows_mine, rows_other, first_ref, second_ref,
    acc_ref, sq_ref, base_ref, scale_ref, first_out, second_out, normed_a, normed_b, first_buf, second_buf, sems,
):
    seqs, kept, _ = mask_ref.shape
    cols = w_ref.shape[1]
    col = pl.multiple_of(tensor_index() * cols, cols)
    even = lax.axis_index("c") == 0

    mine, other = rows_mine[...], rows_other[...]
    summed = jnp.concatenate([jnp.where(even, mine, other), jnp.where(even, other, mine)], axis=2)
    share = summed.shape[1] // 2
    first, second = adam_update(summed, first_ref[:, chip_rows()], second_ref[:, chip_rows()])
    first_buf[...] = jnp.where(even, first[:, :share], first[:, share:])
    second_buf[...] = jnp.where(even, second[:, :share], second[:, share:])
    out = [
        pltpu.make_async_copy(first_buf, first_out, sems.at[0]),
        pltpu.make_async_copy(second_buf, second_out, sems.at[1]),
    ]
    start(out)

    multiply(cuts, x_ref, w_ref, mask_ref, gain_ref, embed_ref, acc_ref, sq_ref, (normed_a, normed_b))
    for seq in range(seqs):
        rows = slice(seq * kept, (seq + 1) * kept)
        mean = jnp.sum(sq_ref[rows], axis=1, keepdims=True) * (1.0 / FEATURES)
        scale = jnp.broadcast_to(lax.rsqrt(mean + norm_epsilon), (kept, 128))
        code = mask_ref[seq]
        scale_ref[rows] = jnp.where(code > 0.5, adapter_scale * scale, 0.0)
        for j in range(cols // 128):
            lanes = slice(j * 128, (j + 1) * 128)
            at = pl.multiple_of(col + j * 128, 128)
            states = x_ref[seq, :, pl.ds(at, 128)].astype(jnp.float32)
            head, states = states[:MIN_PROMPT], states[MIN_PROMPT:]
            hidden = jnp.where(code > 1.5, embed_ref[pl.ds(at // 128, 1)], states)
            value = jnp.where(code > 0.5, hidden + scale * acc_ref[rows, lanes], states)
            base_ref[seq, :MIN_PROMPT, lanes] = head
            base_ref[seq, MIN_PROMPT:, lanes] = value
    wait(out)


VMEM = pl.BlockSpec(memory_space=pltpu.VMEM)
SMEM = pl.BlockSpec(memory_space=pltpu.SMEM)
HBM = pl.BlockSpec(memory_space=pltpu.HBM)
ANY = pl.BlockSpec(memory_space=pl.ANY)


def in_hbm(v):
    return pltpu.with_memory_space_constraint(v, pltpu.HBM)


def in_vmem(v):
    return pltpu.with_memory_space_constraint(v, pltpu.VMEM)


def cost(rows, cols, cuts):
    depth = cuts[-1] - cuts[0]
    return pl.CostEstimate(flops=2 * rows * depth * cols, bytes_accessed=4 * rows * cols, transcendentals=0)


def small_call(kernel, shapes, name, *args, scratch=()):
    in_specs = [ANY if isinstance(v, tuple) else VMEM for v in args]
    args = [v[0] if isinstance(v, tuple) else v for v in args]
    return pl.pallas_call(
        kernel,
        in_specs=in_specs,
        out_specs=[VMEM] * len(shapes),
        out_shape=[jax.ShapeDtypeStruct(*v) for v in shapes],
        scratch_shapes=[pltpu.VMEM(*v) for v in scratch],
        compiler_params=pltpu.CompilerParams(vmem_limit_bytes=4 * MIB),
        name=name,
    )(*args)


def widest(cuts):
    return max(b - a for a, b in zip(cuts, cuts[1:]))


def prepare(prompt_len, bits, gain, embed, x, token, cols, block):
    seqs, length, width = x.shape
    kept = length - MIN_PROMPT
    rows = seqs * kept
    shapes = [
        ((seqs, kept, 128), jnp.float32),
        ((rows, cols // 2), jnp.bfloat16),
        ((rows, cols // 2), jnp.bfloat16),
        (embed.shape, jnp.float32),
        ((rows, 128), jnp.float32),
        ((rows, block), jnp.bfloat16),
    ]
    return pl.pallas_call(
        functools.partial(prepare_kernel, 0),
        in_specs=[VMEM] * 5 + [ANY],
        out_specs=[VMEM] * len(shapes),
        out_shape=[jax.ShapeDtypeStruct(*s) for s in shapes],
        compiler_params=pltpu.CompilerParams(vmem_limit_bytes=8 * MIB),
        name="prepare",
    )(*[in_vmem(v) for v in (prompt_len, bits, gain, embed, x)], token)


def main_first(normed, common, token, sq, cuts):
    mask, gain, embed, x, w = common
    rows, cols = normed.shape[0], w.shape[1]
    scratch = pltpu.VMEM((rows, widest(cuts)), jnp.bfloat16)
    return pl.pallas_call(
        functools.partial(y_kernel, cuts),
        in_specs=[VMEM] * 6 + [ANY, VMEM],
        out_specs=[VMEM] * 2,
        out_shape=[jax.ShapeDtypeStruct((rows, cols), jnp.float32), jax.ShapeDtypeStruct(sq.shape, jnp.float32)],
        input_output_aliases={7: 1},
        scratch_shapes=[scratch, scratch],
        compiler_params=pltpu.CompilerParams(vmem_limit_bytes=12 * MIB),
        cost_estimate=cost(rows, cols, cuts),
        name="main_y",
    )(normed, mask, gain, embed, in_vmem(x), in_vmem(w), token, sq)


def main_part(kernel, name, cuts, common, token, state, extra, extra_specs, shapes, out_specs, scratch=()):
    mask, gain, embed, x, w = common
    rows, cols = state[0].shape
    shapes = [(state[0].shape, jnp.float32), (state[1].shape, jnp.float32), *shapes]
    normed = pltpu.VMEM((rows, widest(cuts)), jnp.bfloat16)
    out = pl.pallas_call(
        functools.partial(kernel, cuts),
        in_specs=[VMEM] * 5 + [ANY] + [VMEM] * 2 + extra_specs,
        out_specs=[VMEM] * 2 + out_specs,
        out_shape=[jax.ShapeDtypeStruct(*s) for s in shapes],
        input_output_aliases={6: 0, 7: 1},
        scratch_shapes=[normed, normed, *scratch],
        compiler_params=pltpu.CompilerParams(vmem_limit_bytes=12 * MIB),
        cost_estimate=cost(rows, cols, cuts),
        name=name,
    )(mask, gain, embed, in_vmem(x), in_vmem(w), token, *state, *extra)
    return out[:2], out[2:]


def add_kernel(mine_ref, theirs_ref, *refs):
    refs[-1][...] = (mine_ref[...].astype(jnp.float32) + theirs_ref[...].astype(jnp.float32)).astype(jnp.bfloat16)


def gather_sum_kernel(mine_ref, r1_ref, r2_ref, r3_ref, _, total_ref, sent_ref):
    total = mine_ref[...] + r1_ref[...].astype(jnp.float32)
    total += r2_ref[...].astype(jnp.float32) + r3_ref[...].astype(jnp.float32)
    total_ref[...] = total
    sent_ref[...] = total.astype(jnp.bfloat16)


def parity():
    return lax.rem(lax.axis_index("y"), 2)


def by_parity(v):
    groups = v.reshape(v.shape[0] // 16, 2, 8, v.shape[1])
    flat = (v.shape[0] // 2, v.shape[1])
    even = parity() == 0
    mine = jnp.where(even, groups[:, 0], groups[:, 1])
    others = jnp.where(even, groups[:, 1], groups[:, 0])
    return mine.reshape(flat), others.reshape(flat)


def from_parity(mine, others):
    shape = (mine.shape[0] // 8, 8, mine.shape[1])
    even = parity() == 0
    mine, others = mine.reshape(shape), others.reshape(shape)
    groups = jnp.stack([jnp.where(even, mine, others), jnp.where(even, others, mine)], axis=1)
    return groups.reshape(2 * shape[0] * 8, shape[2])


def core_sum_kernel(mine_ref, theirs_ref, total_ref, same_ref, flip_ref):
    a = mine_ref[0] + theirs_ref[0].astype(jnp.float32)
    b = mine_ref[1] + theirs_ref[1].astype(jnp.float32)
    mine, others = by_parity(a)
    total = jnp.concatenate([b, mine], axis=0)
    total_ref[...] = total
    same_ref[...] = total.astype(jnp.bfloat16)
    flip_ref[...] = jnp.concatenate([b, others], axis=0).astype(jnp.bfloat16)


def update_kernel(total_ref, theirs_ref, factors_ref, first_ref, second_ref, _, a_ref, b_ref, rows_ref, sum_ref):
    rank, width = b_ref.shape
    at = core_lanes(width)
    total = total_ref[...] + theirs_ref[...].astype(jnp.float32)
    first, second = adam_update(total[:rank], first_ref[1, :, at], second_ref[1, :, at])
    b_ref[...] = factor_update(first, second, factors_ref[1, :, at]).astype(jnp.bfloat16)
    mine = [by_parity(ref[0, :, at])[0] for ref in (factors_ref, first_ref, second_ref)]
    first, second = adam_update(total[rank:], mine[1], mine[2])
    a_ref[...] = factor_update(first, second, mine[0]).astype(jnp.bfloat16)
    sum_ref[...] = total
    group = lax.axis_index("zh") * 2 + lax.axis_index("y") // 2
    rows_ref[0] = sum_ref[pl.ds(pl.multiple_of(rank + group * 8, 8), 8)]
    rows_ref[1] = sum_ref[chip_rows()]


ROW_BY_ROW = (((1,), (1,)), ((), ()))


def low_rank_first_kernel(own_ref, mine_ref, out_ref):
    out_ref[...] = lax.dot_general(own_ref[...], mine_ref[...], ROW_BY_ROW, preferred_element_type=jnp.float32)


def low_rank_kernel(first_ref, own_ref, other_ref, out_ref):
    rows, rank = first_ref.shape
    half = out_ref.shape[0]
    prod = lax.dot_general(own_ref[...], other_ref[...], ROW_BY_ROW, preferred_element_type=jnp.float32)
    prod += first_ref[...]
    tail = jnp.concatenate([prod[half:], jnp.zeros((2 * half - rows, rank), jnp.float32)], axis=0)
    out_ref[...] = jnp.concatenate([prod[:half], tail], axis=1).astype(jnp.bfloat16)


def join_kernel(a_mine, a_core, a_y, a_y_core, _, a_ref):
    mine = from_parity(a_mine[...].astype(jnp.float32), a_y[...].astype(jnp.float32))
    other = from_parity(a_core[...].astype(jnp.float32), a_y_core[...].astype(jnp.float32))
    even = lax.axis_index("c") == 0
    joined = jnp.concatenate([jnp.where(even, mine, other), jnp.where(even, other, mine)], axis=1)
    a_ref[...] = joined.astype(jnp.bfloat16)


def final_kernel(mine_ref, r1_ref, r2_ref, r3_ref, a_ref, base_ref, scale_ref, out_ref, stage_ref, sems):
    seqs, length, _ = base_ref.shape
    kept = length - MIN_PROMPT
    rank = a_ref.shape[0]
    half = mine_ref.shape[0]
    total = mine_ref[...].astype(jnp.float32) + r1_ref[...].astype(jnp.float32)
    total += r2_ref[...].astype(jnp.float32) + r3_ref[...].astype(jnp.float32)
    low = jnp.concatenate([total[:, :rank], total[: seqs * kept - half, rank:]], axis=0)
    low = (low * scale_ref[:, :rank]).astype(jnp.bfloat16)
    a = a_ref[...]
    copies = []
    for seq in range(seqs):
        adapter = jnp.dot(low[seq * kept : (seq + 1) * kept], a, preferred_element_type=jnp.float32)
        for piece in range(length // PIECE):
            rows = slice(piece * PIECE, (piece + 1) * PIECE)
            value = base_ref[seq, rows]
            if rows.stop > MIN_PROMPT:
                lead = max(MIN_PROMPT - rows.start, 0)
                part = value[lead:] + adapter[rows.start + lead - MIN_PROMPT : rows.stop - MIN_PROMPT]
                value = jnp.concatenate([value[:lead], part], axis=0) if lead else part
            stage_ref[seq, rows] = value.astype(jnp.bfloat16)
            at = pl.ds(rows.start, PIECE)
            copy = pltpu.make_async_copy(stage_ref.at[seq, at], out_ref.at[seq, at], sems.at[seq, piece])
            copy.start()
            copies.append(copy)
    wait(copies)


def final(mine, received, a, base, scale):
    return pl.pallas_call(
        final_kernel,
        in_specs=[VMEM] * 7,
        out_specs=HBM,
        out_shape=jax.ShapeDtypeStruct(base.shape, jnp.bfloat16),
        scratch_shapes=[
            pltpu.VMEM(base.shape, jnp.bfloat16),
            pltpu.SemaphoreType.DMA((base.shape[0], base.shape[1] // PIECE)),
        ],
        compiler_params=pltpu.CompilerParams(vmem_limit_bytes=20 * MIB),
        name="final",
    )(mine, *received, a, base, scale)


def local(x, mask_bits, prompt_len, weight, norm_gain, mask_embed, grads, factors, first_moment, second_moment):
    width = x.shape[2]
    cols = weight.shape[1]
    two, rank, _ = factors.shape
    wide, narrow = jnp.float32, jnp.bfloat16
    gain = norm_gain.reshape(width // 128, 128)
    embed = mask_embed.reshape(width // 128, 128)

    own, outgoing = pack(grads)
    from_core = exchange(outgoing, "c", (1,))
    held = (rank + rank // 2, cols // 2)
    total, same, flip = small_call(
        core_sum_kernel, [(held, wide), (held, narrow), (held, narrow)], "sum_c", own, from_core
    )
    from_y = [exchange(v, "y", (k,)) for v, k in ((flip, 3), (same, 2), (flip, 1))]

    mask, own_mine, own_other, embed, sq, normed = prepare(
        prompt_len.reshape(1, -1), mask_bits, gain, embed, x, same, cols, CUTS[0][1]
    )
    common = (mask, gain, embed, x, weight)
    state = main_first(normed, common, same, sq, CUTS[0])
    total, sent = small_call(
        gather_sum_kernel, [(held, wide), (held, narrow)], "sum_y", total, *from_y, (state[1],)
    )
    from_z = exchange(sent, ("zh",), (1,))
    state, _ = main_part(part_kernel, "main_z", CUTS[1], common, sent, state, [], [], [], [])

    params = [in_vmem(v) for v in (factors, first_moment, second_moment)]
    part = (rank, cols // 2)
    half_part = (rank // 2, cols // 2)
    a_half, b_own, rows_own = small_call(
        update_kernel, [(half_part, narrow), (part, narrow), ((two, 8, cols // 2), wide)],
        "update", total, from_z, *params, (state[1],), scratch=[(held, wide)],
    )
    b_other = exchange(b_own, "c", (1,))
    rows = own_mine.shape[0]
    (low,) = small_call(low_rank_first_kernel, [((rows, rank), wide)], "low_rank_first", own_mine, b_own)
    packed = (-(-rows // 32) * 16, 2 * rank)
    (low,) = small_call(low_rank_kernel, [(packed, narrow)], "low_rank", low, own_other, b_other)
    from_zl = exchange(low, ("zl",), (1,))
    a_half, rows_own, _ = lax.optimization_barrier((a_half, rows_own, low))
    a_y = exchange(a_half, "y", (1,))
    rows_other = exchange(rows_own, "c", (1,))
    state, _ = main_part(part_kernel, "main_zl", CUTS[2], common, low, state, [], [], [], [])
    (low,) = small_call(add_kernel, [(low.shape, narrow)], "sum_zl", low, from_zl, (state[1],))
    from_x = [exchange(low, ("x",), (k,)) for k in (3, 2, 1)]
    a_half, a_y, _ = lax.optimization_barrier((a_half, a_y, low))
    a_parts = (a_half, exchange(a_half, "c", (1,)), a_y, exchange(a_y, "c", (1,)))
    four = ((two, 4, cols), wide)
    state, (base, scale, out_first, out_second) = main_part(
        last_kernel, "main_x", CUTS[3], common, low, state, [rows_own, rows_other, *params[1:]], [VMEM] * 4,
        [(x.shape[:2] + (cols,), wide), (state[1].shape, wide), four, four], [VMEM] * 2 + [HBM] * 2,
        [pltpu.VMEM(*four), pltpu.VMEM(*four), pltpu.SemaphoreType.DMA((2,))],
    )
    (a,) = small_call(join_kernel, [((rank, cols), narrow)], "join_a", *a_parts, (scale,))
    out = final(low, from_x, a, base, scale)
    return out, out_first, out_second


def solution(mesh):
    split = Mesh(mesh.devices.reshape(2, 4, 2, 4, 2), ("zh", "y", "c", "x", "zl"))
    placed = (
        P(DP, None, None),
        P(DP, None),
        P(DP),
        P(None, TENSOR),
        P(),
        P(),
        P(DP, None, None, TENSOR),
        P(None, None, TENSOR),
        P(None, None, TENSOR),
        P(None, None, TENSOR),
    )
    return jax.shard_map(
        local,
        mesh=split,
        in_specs=placed,
        out_specs=(P(DP, None, TENSOR), P(None, DP, TENSOR), P(None, DP, TENSOR)),
        check_vma=False,
    )
```

```python
import functools
import itertools

import jax
import jax.numpy as jnp
from jax import lax
from jax.experimental import pallas as pl
from jax.experimental.pallas import tpu as pltpu
from jax.sharding import Mesh, PartitionSpec as P

beta_one = 0.9
beta_two = 0.999
learn_rate = 0.03
adam_count = 100
epsilon = 1e-08
adapter_scale = 2.0
norm_epsilon = 1e-05

SIZES = {"zh": 2, "y": 4, "c": 2, "x": 4, "zl": 2}
DP = ("zh", "y", "c")
TENSOR = ("x", "zl")
CUTS = ((0, 1024, 2048, 3072), (3072, 4096, 4864), (4864, 5376), (5376, 6400, 7424, 8192))
FEATURES = 8192
MIN_PROMPT = 24
SKIP = 16
PIECE = 96
MIB = 1 << 20


def f32(v):
    return v.astype(jnp.float32)


def bf16(v):
    return v.astype(jnp.bfloat16)


def exchange(v, axes, key):
    ids = list(itertools.product(*[range(SIZES[a]) for a in axes]))
    index = {t: i for i, t in enumerate(ids)}
    pairs = [(index[t], index[tuple(a ^ k for a, k in zip(t, key))]) for t in ids]
    return lax.ppermute(v, tuple(axes), pairs)


def adam_update(summed_grad, first_moment, second_moment):
    new_first = beta_one * first_moment + (1.0 - beta_one) * summed_grad
    new_second = beta_two * second_moment + (1.0 - beta_two) * summed_grad * summed_grad
    return new_first, new_second


def factor_update(new_first, new_second, param_rows):
    step_size = learn_rate / (1.0 - beta_one**adam_count)
    divisor = jnp.sqrt(new_second / (1.0 - beta_two**adam_count)) + epsilon
    return param_rows - step_size * new_first / divisor


def normalise(x_ref, mask_ref, gain_ref, embed_ref, k0, normed_ref, sq_ref, first):
    seqs, kept, _ = mask_ref.shape
    for seq in range(seqs):
        rows = slice(seq * kept, (seq + 1) * kept)
        squares = None if first else sq_ref[rows]
        for j in range(normed_ref.shape[1] // 128):
            block = k0 // 128 + j
            states = x_ref[seq, SKIP:, k0 + j * 128 : k0 + (j + 1) * 128].astype(jnp.float32)[MIN_PROMPT - SKIP :]
            hidden = jnp.where(mask_ref[seq] > 1.5, embed_ref[block : block + 1], states)
            squares = hidden * hidden if squares is None else squares + hidden * hidden
            normed_ref[rows, j * 128 : (j + 1) * 128] = (hidden * gain_ref[block : block + 1]).astype(jnp.bfloat16)
        sq_ref[rows] = squares


def multiply(cuts, x_ref, w_ref, mask_ref, gain_ref, embed_ref, acc_ref, sq_ref, normed, begun=None):
    def block(i):
        if i == 0 and begun is not None:
            return begun
        return normed[i % 2].at[:, : cuts[i + 1] - cuts[i]]

    def ready(i):
        normalise(x_ref, mask_ref, gain_ref, embed_ref, cuts[i], block(i), sq_ref, False)

    count = len(cuts) - 1
    if begun is None:
        ready(0)
    for i in range(count):
        if i + 1 < count:
            ready(i + 1)
        product = jnp.dot(block(i)[...], w_ref[cuts[i] : cuts[i + 1]], preferred_element_type=jnp.float32)
        if i == 0 and begun is not None:
            acc_ref[...] = product
        else:
            acc_ref[...] += product


def start(copies):
    for copy in copies:
        copy.start()


def wait(copies):
    for copy in copies:
        copy.wait()


def tensor_index():
    return lax.axis_index("x") * 2 + lax.axis_index("zl")


def pack_kernel(grad_ref, own_ref, other_ref, wide_ref, sems):
    width = own_ref.shape[2]
    core = lax.axis_index("c")
    near = pl.ds(pl.multiple_of(core * width, width), width)
    far = pl.ds(pl.multiple_of((1 - core) * width, width), width)
    other = pltpu.make_async_copy(grad_ref.at[0, :, :, far], wide_ref, sems.at[0])
    own = pltpu.make_async_copy(grad_ref.at[0, :, :, near], own_ref, sems.at[1])
    other.start()
    own.start()
    other.wait()
    other_ref[...] = wide_ref[...].astype(jnp.bfloat16)
    own.wait()


def pack(grads):
    _, two, rank, cols = grads.shape
    shape = (two, rank, cols // 2)
    return pl.pallas_call(
        pack_kernel,
        in_specs=[HBM],
        out_specs=[VMEM, VMEM],
        out_shape=[jax.ShapeDtypeStruct(shape, jnp.float32), jax.ShapeDtypeStruct(shape, jnp.bfloat16)],
        scratch_shapes=[pltpu.VMEM(shape, jnp.float32), pltpu.SemaphoreType.DMA((2,))],
        compiler_params=pltpu.CompilerParams(vmem_limit_bytes=8 * MIB),
        cost_estimate=pl.CostEstimate(flops=20_000_000_000, bytes_accessed=80_000_000, transcendentals=0),
        name="pack",
    )(in_hbm(grads))


def prepare_kernel(
    first_block, prompt_ref, bits_ref, gain_ref, embed_ref, x_ref, _, mask_ref, mine_ref, other_ref, embed_out, sq_ref,
    normed_ref, rest_ref,
):
    seqs, kept, _ = mask_ref.shape
    width = mine_ref.shape[1]
    col = pl.multiple_of(tensor_index() * 2 * width, 2 * width)
    core = lax.axis_index("c")
    embed_out[...] = embed_ref[...].astype(jnp.float32)
    length = bits_ref.shape[1]
    here = lax.broadcasted_iota(jnp.int32, (kept, length), 0) + MIN_PROMPT
    there = lax.broadcasted_iota(jnp.int32, (kept, length), 1)
    position = lax.broadcasted_iota(jnp.int32, (kept, 1), 0) + MIN_PROMPT
    for seq in range(seqs):
        bits = jnp.where(here == there, bits_ref[seq : seq + 1, :], 0)
        chosen = 1.0 + jnp.sum((bits == 1).astype(jnp.float32), axis=1, keepdims=True)
        column = jnp.where(position >= prompt_ref[0:1, seq : seq + 1], chosen, 0.0)
        mask_ref[seq] = jnp.broadcast_to(column, (kept, 128))

    for at_core, dst in ((core, mine_ref), (1 - core, other_ref)):
        for seq in range(seqs):
            rows = slice(seq * kept, (seq + 1) * kept)
            for j in range(width // 128):
                at = pl.multiple_of(at_core * width + j * 128, 128)
                lanes = pl.ds(at, 128)
                block = pl.ds((col + at) // 128, 1)
                states = x_ref[seq, :, pl.ds(pl.multiple_of(col + at, 128), 128)].astype(jnp.float32)
                hidden = jnp.where(mask_ref[seq] > 1.5, embed_out[block], states[MIN_PROMPT:])
                rest_ref[seq, :MIN_PROMPT, lanes] = states[:MIN_PROMPT]
                rest_ref[seq, MIN_PROMPT:, lanes] = hidden
                dst[rows, j * 128 : (j + 1) * 128] = (hidden * gain_ref[block]).astype(jnp.bfloat16)
    normalise(x_ref, mask_ref, gain_ref, embed_out, first_block, normed_ref, sq_ref, True)


def y_kernel(
    cuts, normed_in, mask_ref, gain_ref, embed_ref, x_ref, w_ref, _, sq_in, acc_ref, sq_ref, normed_a, normed_b
):
    multiply(cuts, x_ref, w_ref, mask_ref, gain_ref, embed_ref, acc_ref, sq_ref, (normed_a, normed_b), normed_in)


def chip_rows():
    return pl.ds(pl.multiple_of((lax.axis_index("zh") * 4 + lax.axis_index("y")) * 8, 8), 8)


def core_lanes(width):
    return pl.ds(pl.multiple_of(lax.axis_index("c") * width, width), width)


def part_kernel(
    cuts, mask_ref, gain_ref, embed_ref, x_ref, w_ref, _, acc_in, sq_in, acc_ref, sq_ref, normed_a, normed_b
):
    multiply(cuts, x_ref, w_ref, mask_ref, gain_ref, embed_ref, acc_ref, sq_ref, (normed_a, normed_b))


def last_kernel(
    cuts, mask_ref, gain_ref, embed_ref, x_ref, w_ref, _, acc_in, sq_in, rows_mine, rows_other, first_ref, second_ref,
    acc_ref, sq_ref, scale_ref, first_out, second_out, normed_a, normed_b,
):
    seqs, kept, _ = mask_ref.shape
    even = lax.axis_index("c") == 0

    args = (x_ref, w_ref, mask_ref, gain_ref, embed_ref, acc_ref, sq_ref, (normed_a, normed_b))
    multiply(cuts[:2], *args)
    mine, other = rows_mine[...], rows_other[...]
    summed = jnp.concatenate([jnp.where(even, mine, other), jnp.where(even, other, mine)], axis=2)
    share = summed.shape[1] // 2
    first, second = adam_update(summed, first_ref[:, chip_rows()], second_ref[:, chip_rows()])
    first_out[...] = jnp.where(even, first[:, :share], first[:, share:])
    second_out[...] = jnp.where(even, second[:, :share], second[:, share:])
    multiply(cuts[1:], *args)
    for seq in range(seqs):
        rows = slice(seq * kept, (seq + 1) * kept)
        mean = jnp.sum(sq_ref[rows], axis=1, keepdims=True) * (1.0 / FEATURES)
        scale = jnp.broadcast_to(lax.rsqrt(mean + norm_epsilon), (kept, 128))
        scale_ref[rows] = jnp.where(mask_ref[seq] > 0.5, scale, 0.0)


VMEM = pl.BlockSpec(memory_space=pltpu.VMEM)
SMEM = pl.BlockSpec(memory_space=pltpu.SMEM)
HBM = pl.BlockSpec(memory_space=pltpu.HBM)
ANY = pl.BlockSpec(memory_space=pl.ANY)


def in_hbm(v):
    return pltpu.with_memory_space_constraint(v, pltpu.HBM)


def in_vmem(v):
    return pltpu.with_memory_space_constraint(v, pltpu.VMEM)


def cost(rows, cols, cuts):
    depth = cuts[-1] - cuts[0]
    return pl.CostEstimate(flops=2 * rows * depth * cols, bytes_accessed=4 * rows * cols, transcendentals=0)


def small_call(kernel, shapes, name, *args, scratch=()):
    in_specs = [ANY if isinstance(v, tuple) else VMEM for v in args]
    args = [v[0] if isinstance(v, tuple) else v for v in args]
    return pl.pallas_call(
        kernel,
        in_specs=in_specs,
        out_specs=[VMEM] * len(shapes),
        out_shape=[jax.ShapeDtypeStruct(*v) for v in shapes],
        scratch_shapes=[pltpu.VMEM(*v) for v in scratch],
        compiler_params=pltpu.CompilerParams(vmem_limit_bytes=4 * MIB),
        name=name,
    )(*args)


def widest(cuts):
    return max(b - a for a, b in zip(cuts, cuts[1:]))


def prepare(prompt_len, bits, gain, embed, x, token, cols, block):
    seqs, length, width = x.shape
    kept = length - MIN_PROMPT
    rows = seqs * kept
    shapes = [
        ((seqs, kept, 128), jnp.float32),
        ((rows, cols // 2), jnp.bfloat16),
        ((rows, cols // 2), jnp.bfloat16),
        (embed.shape, jnp.float32),
        ((rows, 128), jnp.float32),
        ((rows, block), jnp.bfloat16),
        ((seqs, length, cols), jnp.float32),
    ]
    return pl.pallas_call(
        functools.partial(prepare_kernel, 0),
        in_specs=[VMEM] * 5 + [ANY],
        out_specs=[VMEM] * len(shapes),
        out_shape=[jax.ShapeDtypeStruct(*s) for s in shapes],
        compiler_params=pltpu.CompilerParams(vmem_limit_bytes=8 * MIB),
        name="prepare",
    )(*[in_vmem(v) for v in (prompt_len, bits, gain, embed, x)], token)


def main_first(normed, common, token, sq, cuts):
    mask, gain, embed, x, w = common
    rows, cols = normed.shape[0], w.shape[1]
    scratch = pltpu.VMEM((rows, widest(cuts)), jnp.bfloat16)
    return pl.pallas_call(
        functools.partial(y_kernel, cuts),
        in_specs=[VMEM] * 6 + [ANY, VMEM],
        out_specs=[VMEM] * 2,
        out_shape=[jax.ShapeDtypeStruct((rows, cols), jnp.float32), jax.ShapeDtypeStruct(sq.shape, jnp.float32)],
        input_output_aliases={7: 1},
        scratch_shapes=[scratch, scratch],
        compiler_params=pltpu.CompilerParams(vmem_limit_bytes=12 * MIB),
        cost_estimate=cost(rows, cols, cuts),
        name="main_y",
    )(normed, mask, gain, embed, in_vmem(x), in_vmem(w), token, sq)


def main_part(kernel, name, cuts, common, token, state, extra, extra_specs, shapes, out_specs, scratch=()):
    mask, gain, embed, x, w = common
    rows, cols = state[0].shape
    shapes = [(state[0].shape, jnp.float32), (state[1].shape, jnp.float32), *shapes]
    normed = pltpu.VMEM((rows, widest(cuts)), jnp.bfloat16)
    out = pl.pallas_call(
        functools.partial(kernel, cuts),
        in_specs=[VMEM] * 5 + [ANY] + [VMEM] * 2 + extra_specs,
        out_specs=[VMEM] * 2 + out_specs,
        out_shape=[jax.ShapeDtypeStruct(*s) for s in shapes],
        input_output_aliases={6: 0, 7: 1},
        scratch_shapes=[normed, normed, *scratch],
        compiler_params=pltpu.CompilerParams(vmem_limit_bytes=12 * MIB),
        cost_estimate=cost(rows, cols, cuts),
        name=name,
    )(mask, gain, embed, in_vmem(x), in_vmem(w), token, *state, *extra)
    return out[:2], out[2:]


def add_kernel(mine_ref, theirs_ref, *refs):
    refs[-1][...] = (mine_ref[...].astype(jnp.float32) + theirs_ref[...].astype(jnp.float32)).astype(jnp.bfloat16)


def gather_sum_kernel(mine_ref, r1_ref, r2_ref, r3_ref, _, total_ref, sent_ref):
    total = mine_ref[...] + r1_ref[...].astype(jnp.float32)
    total += r2_ref[...].astype(jnp.float32) + r3_ref[...].astype(jnp.float32)
    total_ref[...] = total
    sent_ref[...] = total.astype(jnp.bfloat16)


def parity():
    return lax.rem(lax.axis_index("y"), 2)


def by_parity(v):
    groups = v.reshape(v.shape[0] // 16, 2, 8, v.shape[1])
    flat = (v.shape[0] // 2, v.shape[1])
    even = parity() == 0
    mine = jnp.where(even, groups[:, 0], groups[:, 1])
    others = jnp.where(even, groups[:, 1], groups[:, 0])
    return mine.reshape(flat), others.reshape(flat)


def from_parity(mine, others):
    shape = (mine.shape[0] // 8, 8, mine.shape[1])
    even = parity() == 0
    mine, others = mine.reshape(shape), others.reshape(shape)
    groups = jnp.stack([jnp.where(even, mine, others), jnp.where(even, others, mine)], axis=1)
    return groups.reshape(2 * shape[0] * 8, shape[2])


def core_sum_kernel(mine_ref, theirs_ref, total_ref, same_ref, flip_ref):
    a = mine_ref[0] + theirs_ref[0].astype(jnp.float32)
    b = mine_ref[1] + theirs_ref[1].astype(jnp.float32)
    mine, others = by_parity(a)
    total = jnp.concatenate([b, mine], axis=0)
    total_ref[...] = total
    same_ref[...] = total.astype(jnp.bfloat16)
    flip_ref[...] = jnp.concatenate([b, others], axis=0).astype(jnp.bfloat16)


def update_kernel(total_ref, theirs_ref, factors_ref, first_ref, second_ref, _, a_ref, b_ref, rows_ref, sum_ref):
    rank, width = b_ref.shape
    at = core_lanes(width)
    total = total_ref[...] + theirs_ref[...].astype(jnp.float32)
    first, second = adam_update(total[:rank], first_ref[1, :, at], second_ref[1, :, at])
    b_ref[...] = factor_update(first, second, factors_ref[1, :, at]).astype(jnp.bfloat16)
    mine = [by_parity(ref[0, :, at])[0] for ref in (factors_ref, first_ref, second_ref)]
    first, second = adam_update(total[rank:], mine[1], mine[2])
    a_ref[...] = factor_update(first, second, mine[0]).astype(jnp.bfloat16)
    sum_ref[...] = total
    group = lax.axis_index("zh") * 2 + lax.axis_index("y") // 2
    rows_ref[0] = sum_ref[pl.ds(pl.multiple_of(rank + group * 8, 8), 8)]
    rows_ref[1] = sum_ref[chip_rows()]


ROW_BY_ROW = (((1,), (1,)), ((), ()))


def low_rank_first_kernel(own_ref, mine_ref, out_ref):
    out_ref[...] = lax.dot_general(own_ref[...], mine_ref[...], ROW_BY_ROW, preferred_element_type=jnp.float32)


def low_rank_kernel(first_ref, own_ref, other_ref, out_ref):
    rows, rank = first_ref.shape
    half = out_ref.shape[0]
    prod = lax.dot_general(own_ref[...], other_ref[...], ROW_BY_ROW, preferred_element_type=jnp.float32)
    prod += first_ref[...]
    tail = jnp.concatenate([prod[half:], jnp.zeros((2 * half - rows, rank), jnp.float32)], axis=0)
    out_ref[...] = jnp.concatenate([prod[:half], tail], axis=1).astype(jnp.bfloat16)


def pair_kernel(mine_ref, other_ref, _, out_ref):
    out_ref[...] = jnp.concatenate([mine_ref[...], other_ref[...]], axis=0)


def join_kernel(here_ref, there_ref, _, a_ref):
    here, there = here_ref[...].astype(jnp.float32), there_ref[...].astype(jnp.float32)
    half = here.shape[0] // 2
    mine, other = from_parity(here[:half], there[:half]), from_parity(here[half:], there[half:])
    even = lax.axis_index("c") == 0
    joined = jnp.concatenate([jnp.where(even, mine, other), jnp.where(even, other, mine)], axis=1)
    a_ref[...] = joined.astype(jnp.bfloat16)


def final_kernel(
    mine_ref, r1_ref, r2_ref, r3_ref, a_ref, rest_ref, acc_ref, scale_ref, first_ref, second_ref,
    out_ref, first_out, second_out, stage_ref, sems, moment_sems,
):
    copies = [
        pltpu.make_async_copy(first_ref, first_out, moment_sems.at[0]),
        pltpu.make_async_copy(second_ref, second_out, moment_sems.at[1]),
    ]
    start(copies)
    seqs, length, cols = rest_ref.shape
    kept = length - MIN_PROMPT
    rank = a_ref.shape[0]
    half = mine_ref.shape[0]
    total = mine_ref[...].astype(jnp.float32) + r1_ref[...].astype(jnp.float32)
    total += r2_ref[...].astype(jnp.float32) + r3_ref[...].astype(jnp.float32)
    low = jnp.concatenate([total[:, :rank], total[: seqs * kept - half, rank:]], axis=0)
    low = (low * (adapter_scale * scale_ref[:, :rank])).astype(jnp.bfloat16)
    a = a_ref[...]
    for seq in range(seqs):
        adapter = jnp.dot(low[seq * kept : (seq + 1) * kept], a, preferred_element_type=jnp.float32)
        for piece in range(length // PIECE):
            begin, end = piece * PIECE, (piece + 1) * PIECE
            lead = max(MIN_PROMPT - begin, 0)
            own = slice(begin + lead - MIN_PROMPT, end - MIN_PROMPT)
            rows = slice(seq * kept + own.start, seq * kept + own.stop)
            for j in range(cols // 128):
                lanes = slice(j * 128, (j + 1) * 128)
                value = rest_ref[seq, begin + lead : end, lanes] + scale_ref[rows] * acc_ref[rows, lanes]
                value += adapter[own, lanes]
                if lead:
                    value = jnp.concatenate([rest_ref[seq, begin : begin + lead, lanes], value], axis=0)
                stage_ref[seq, begin:end, lanes] = value.astype(jnp.bfloat16)
            at = pl.ds(begin, PIECE)
            copy = pltpu.make_async_copy(stage_ref.at[seq, at], out_ref.at[seq, at], sems.at[seq, piece])
            copy.start()
            copies.append(copy)
    wait(copies)


def final(mine, received, a, rest, acc, scale, moments):
    return pl.pallas_call(
        final_kernel,
        in_specs=[VMEM] * 10,
        out_specs=[HBM] * 3,
        out_shape=[
            jax.ShapeDtypeStruct(rest.shape, jnp.bfloat16),
            *[jax.ShapeDtypeStruct(v.shape, jnp.float32) for v in moments],
        ],
        scratch_shapes=[
            pltpu.VMEM(rest.shape, jnp.bfloat16),
            pltpu.SemaphoreType.DMA((rest.shape[0], rest.shape[1] // PIECE)),
            pltpu.SemaphoreType.DMA((2,)),
        ],
        compiler_params=pltpu.CompilerParams(vmem_limit_bytes=16 * MIB),
        name="final",
    )(mine, *received, a, rest, acc, scale, *moments)


def local(x, mask_bits, prompt_len, weight, norm_gain, mask_embed, grads, factors, first_moment, second_moment):
    width = x.shape[2]
    cols = weight.shape[1]
    two, rank, _ = factors.shape
    wide, narrow = jnp.float32, jnp.bfloat16
    gain = norm_gain.reshape(width // 128, 128)
    embed = mask_embed.reshape(width // 128, 128)

    own, outgoing = pack(grads)
    from_core = exchange(outgoing, "c", (1,))
    held = (rank + rank // 2, cols // 2)
    total, same, flip = small_call(
        core_sum_kernel, [(held, wide), (held, narrow), (held, narrow)], "sum_c", own, from_core
    )
    from_y = [exchange(v, "y", (k,)) for v, k in ((flip, 1), (flip, 3), (same, 2))]

    mask, own_mine, own_other, embed, sq, normed, rest = prepare(
        prompt_len.reshape(1, -1), mask_bits, gain, embed, x, same, cols, CUTS[0][1]
    )
    common = (mask, gain, embed, x, weight)
    state = main_first(normed, common, same, sq, CUTS[0])
    total, sent = small_call(
        gather_sum_kernel, [(held, wide), (held, narrow)], "sum_y", total, *from_y, (state[1],)
    )
    from_z = exchange(sent, ("zh",), (1,))
    state, _ = main_part(part_kernel, "main_z", CUTS[1], common, sent, state, [], [], [], [])

    params = [in_vmem(v) for v in (factors, first_moment, second_moment)]
    part = (rank, cols // 2)
    half_part = (rank // 2, cols // 2)
    a_half, b_own, rows_own = small_call(
        update_kernel, [(half_part, narrow), (part, narrow), ((two, 8, cols // 2), wide)],
        "update", total, from_z, *params, (state[1],), scratch=[(held, wide)],
    )
    b_other = exchange(b_own, "c", (1,))
    a_core = exchange(a_half, "c", (1,))
    rows_other = exchange(rows_own, "c", (1,))
    rows = own_mine.shape[0]
    (low,) = small_call(low_rank_first_kernel, [((rows, rank), wide)], "low_rank_first", own_mine, b_own)
    packed = (-(-rows // 32) * 16, 2 * rank)
    (low,) = small_call(low_rank_kernel, [(packed, narrow)], "low_rank", low, own_other, b_other)
    from_zl = exchange(low, ("zl",), (1,))
    (a_here,) = small_call(pair_kernel, [(part, narrow)], "pair_a", a_half, a_core, (low,))
    a_there = exchange(a_here, "y", (1,))
    state, _ = main_part(part_kernel, "main_zl", CUTS[2], common, low, state, [], [], [], [])
    (low,) = small_call(add_kernel, [(low.shape, narrow)], "sum_zl", low, from_zl, (state[1],))
    from_x = [exchange(low, ("x",), (k,)) for k in (1, 3, 2)]
    four = ((two, 4, cols), wide)
    state, (scale, *moments) = main_part(
        last_kernel, "main_x", CUTS[3], common, low, state, [rows_own, rows_other, *params[1:]], [VMEM] * 4,
        [(state[1].shape, wide), four, four], [VMEM] * 3,
    )
    (a,) = small_call(join_kernel, [((rank, cols), narrow)], "join_a", a_here, a_there, (scale,))
    return final(low, from_x, a, rest, state[0], scale, moments)


def solution(mesh):
    split = Mesh(mesh.devices.reshape(2, 4, 2, 4, 2), ("zh", "y", "c", "x", "zl"))
    placed = (
        P(DP, None, None),
        P(DP, None),
        P(DP),
        P(None, TENSOR),
        P(),
        P(),
        P(DP, None, None, TENSOR),
        P(None, None, TENSOR),
        P(None, None, TENSOR),
        P(None, None, TENSOR),
    )
    return jax.shard_map(
        local,
        mesh=split,
        in_specs=placed,
        out_specs=(P(DP, None, TENSOR), P(None, DP, TENSOR), P(None, DP, TENSOR)),
        check_vma=False,
    )
```

```python
import functools
import itertools

import jax
import jax.numpy as jnp
from jax import lax
from jax.experimental import pallas as pl
from jax.experimental.pallas import tpu as pltpu
from jax.sharding import Mesh, PartitionSpec as P

beta_one = 0.9
beta_two = 0.999
learn_rate = 0.03
adam_count = 100
epsilon = 1e-08
adapter_scale = 2.0
norm_epsilon = 1e-05

SIZES = {"zh": 2, "y": 4, "c": 2, "x": 4, "zl": 2}
DP = ("zh", "y", "c")
TENSOR = ("x", "zl")
CUTS = ((0, 1024, 2048, 3072), (3072, 4096, 4864), (4864, 5632), (5632, 6656, 7680, 8192))
FEATURES = 8192
MIN_PROMPT = 24
SKIP = 16
PIECE = 96
MIB = 1 << 20


def f32(v):
    return v.astype(jnp.float32)


def bf16(v):
    return v.astype(jnp.bfloat16)


def exchange(v, axes, key):
    ids = list(itertools.product(*[range(SIZES[a]) for a in axes]))
    index = {t: i for i, t in enumerate(ids)}
    pairs = [(index[t], index[tuple(a ^ k for a, k in zip(t, key))]) for t in ids]
    return lax.ppermute(v, tuple(axes), pairs)


def adam_update(summed_grad, first_moment, second_moment):
    new_first = beta_one * first_moment + (1.0 - beta_one) * summed_grad
    new_second = beta_two * second_moment + (1.0 - beta_two) * summed_grad * summed_grad
    return new_first, new_second


def factor_update(new_first, new_second, param_rows):
    step_size = learn_rate / (1.0 - beta_one**adam_count)
    divisor = jnp.sqrt(new_second / (1.0 - beta_two**adam_count)) + epsilon
    return param_rows - step_size * new_first / divisor


def normalise(x_ref, mask_ref, gain_ref, embed_ref, k0, normed_ref, sq_ref, first):
    seqs, kept, _ = mask_ref.shape
    for seq in range(seqs):
        rows = slice(seq * kept, (seq + 1) * kept)
        squares = None if first else sq_ref[rows]
        for j in range(normed_ref.shape[1] // 128):
            block = k0 // 128 + j
            states = x_ref[seq, SKIP:, k0 + j * 128 : k0 + (j + 1) * 128].astype(jnp.float32)[MIN_PROMPT - SKIP :]
            hidden = jnp.where(mask_ref[seq] > 1.5, embed_ref[block : block + 1], states)
            squares = hidden * hidden if squares is None else squares + hidden * hidden
            normed_ref[rows, j * 128 : (j + 1) * 128] = (hidden * gain_ref[block : block + 1]).astype(jnp.bfloat16)
        sq_ref[rows] = squares


def multiply(cuts, x_ref, w_ref, mask_ref, gain_ref, embed_ref, acc_ref, sq_ref, normed, begun=None):
    def block(i):
        if i == 0 and begun is not None:
            return begun
        return normed[i % 2].at[:, : cuts[i + 1] - cuts[i]]

    def ready(i):
        normalise(x_ref, mask_ref, gain_ref, embed_ref, cuts[i], block(i), sq_ref, False)

    count = len(cuts) - 1
    if begun is None:
        ready(0)
    for i in range(count):
        if i + 1 < count:
            ready(i + 1)
        product = jnp.dot(block(i)[...], w_ref[cuts[i] : cuts[i + 1]], preferred_element_type=jnp.float32)
        if i == 0 and begun is not None:
            acc_ref[...] = product
        else:
            acc_ref[...] += product


def start(copies):
    for copy in copies:
        copy.start()


def wait(copies):
    for copy in copies:
        copy.wait()


def tensor_index():
    return lax.axis_index("x") * 2 + lax.axis_index("zl")


def pack_kernel(grad_ref, own_ref, other_ref, wide_ref, sems):
    width = own_ref.shape[2]
    core = lax.axis_index("c")
    near = pl.ds(pl.multiple_of(core * width, width), width)
    far = pl.ds(pl.multiple_of((1 - core) * width, width), width)
    other = pltpu.make_async_copy(grad_ref.at[0, :, :, far], wide_ref, sems.at[0])
    own = pltpu.make_async_copy(grad_ref.at[0, :, :, near], own_ref, sems.at[1])
    other.start()
    own.start()
    other.wait()
    other_ref[...] = wide_ref[...].astype(jnp.bfloat16)
    own.wait()


def pack(grads):
    _, two, rank, cols = grads.shape
    shape = (two, rank, cols // 2)
    return pl.pallas_call(
        pack_kernel,
        in_specs=[HBM],
        out_specs=[VMEM, VMEM],
        out_shape=[jax.ShapeDtypeStruct(shape, jnp.float32), jax.ShapeDtypeStruct(shape, jnp.bfloat16)],
        scratch_shapes=[pltpu.VMEM(shape, jnp.float32), pltpu.SemaphoreType.DMA((2,))],
        compiler_params=pltpu.CompilerParams(vmem_limit_bytes=8 * MIB),
        cost_estimate=pl.CostEstimate(flops=20_000_000_000, bytes_accessed=80_000_000, transcendentals=0),
        name="pack",
    )(in_hbm(grads))


def prepare_kernel(
    first_block, prompt_ref, bits_ref, gain_ref, embed_ref, x_ref, _, mask_ref, mine_ref, other_ref, embed_out, sq_ref,
    normed_ref, rest_ref,
):
    seqs, kept, _ = mask_ref.shape
    width = mine_ref.shape[1]
    col = pl.multiple_of(tensor_index() * 2 * width, 2 * width)
    core = lax.axis_index("c")
    embed_out[...] = embed_ref[...].astype(jnp.float32)
    length = bits_ref.shape[1]
    here = lax.broadcasted_iota(jnp.int32, (kept, length), 0) + MIN_PROMPT
    there = lax.broadcasted_iota(jnp.int32, (kept, length), 1)
    position = lax.broadcasted_iota(jnp.int32, (kept, 1), 0) + MIN_PROMPT
    for seq in range(seqs):
        bits = jnp.where(here == there, bits_ref[seq : seq + 1, :], 0)
        chosen = 1.0 + jnp.sum((bits == 1).astype(jnp.float32), axis=1, keepdims=True)
        column = jnp.where(position >= prompt_ref[0:1, seq : seq + 1], chosen, 0.0)
        mask_ref[seq] = jnp.broadcast_to(column, (kept, 128))

    for at_core, dst in ((core, mine_ref), (1 - core, other_ref)):
        for seq in range(seqs):
            rows = slice(seq * kept, (seq + 1) * kept)
            for j in range(width // 128):
                at = pl.multiple_of(at_core * width + j * 128, 128)
                lanes = pl.ds(at, 128)
                block = pl.ds((col + at) // 128, 1)
                states = x_ref[seq, :, pl.ds(pl.multiple_of(col + at, 128), 128)].astype(jnp.float32)
                hidden = jnp.where(mask_ref[seq] > 1.5, embed_out[block], states[MIN_PROMPT:])
                rest_ref[seq, :MIN_PROMPT, lanes] = states[:MIN_PROMPT]
                rest_ref[seq, MIN_PROMPT:, lanes] = hidden
                dst[rows, j * 128 : (j + 1) * 128] = (hidden * gain_ref[block]).astype(jnp.bfloat16)
    normalise(x_ref, mask_ref, gain_ref, embed_out, first_block, normed_ref, sq_ref, True)


def y_kernel(
    cuts, normed_in, mask_ref, gain_ref, embed_ref, x_ref, w_ref, _, sq_in, acc_ref, sq_ref, normed_a, normed_b
):
    multiply(cuts, x_ref, w_ref, mask_ref, gain_ref, embed_ref, acc_ref, sq_ref, (normed_a, normed_b), normed_in)


def chip_rows():
    return pl.ds(pl.multiple_of((lax.axis_index("zh") * 4 + lax.axis_index("y")) * 8, 8), 8)


def core_lanes(width):
    return pl.ds(pl.multiple_of(lax.axis_index("c") * width, width), width)


def part_kernel(
    cuts, mask_ref, gain_ref, embed_ref, x_ref, w_ref, _, acc_in, sq_in, acc_ref, sq_ref, normed_a, normed_b
):
    multiply(cuts, x_ref, w_ref, mask_ref, gain_ref, embed_ref, acc_ref, sq_ref, (normed_a, normed_b))


def last_kernel(
    cuts, mask_ref, gain_ref, embed_ref, x_ref, w_ref, _, acc_in, sq_in, rows_mine, rows_other, first_ref, second_ref,
    acc_ref, sq_ref, scale_ref, first_out, second_out, normed_a, normed_b,
):
    seqs, kept, _ = mask_ref.shape
    even = lax.axis_index("c") == 0

    args = (x_ref, w_ref, mask_ref, gain_ref, embed_ref, acc_ref, sq_ref, (normed_a, normed_b))
    multiply(cuts[:2], *args)
    mine, other = rows_mine[...], rows_other[...]
    summed = jnp.concatenate([jnp.where(even, mine, other), jnp.where(even, other, mine)], axis=2)
    share = summed.shape[1] // 2
    first, second = adam_update(summed, first_ref[:, chip_rows()], second_ref[:, chip_rows()])
    first_out[...] = jnp.where(even, first[:, :share], first[:, share:])
    second_out[...] = jnp.where(even, second[:, :share], second[:, share:])
    multiply(cuts[1:], *args)
    for seq in range(seqs):
        rows = slice(seq * kept, (seq + 1) * kept)
        mean = jnp.sum(sq_ref[rows], axis=1, keepdims=True) * (1.0 / FEATURES)
        scale = jnp.broadcast_to(lax.rsqrt(mean + norm_epsilon), (kept, 128))
        scale_ref[rows] = jnp.where(mask_ref[seq] > 0.5, scale, 0.0)


VMEM = pl.BlockSpec(memory_space=pltpu.VMEM)
SMEM = pl.BlockSpec(memory_space=pltpu.SMEM)
HBM = pl.BlockSpec(memory_space=pltpu.HBM)
ANY = pl.BlockSpec(memory_space=pl.ANY)


def in_hbm(v):
    return pltpu.with_memory_space_constraint(v, pltpu.HBM)


def in_vmem(v):
    return pltpu.with_memory_space_constraint(v, pltpu.VMEM)


def cost(rows, cols, cuts):
    depth = cuts[-1] - cuts[0]
    return pl.CostEstimate(flops=2 * rows * depth * cols, bytes_accessed=4 * rows * cols, transcendentals=0)


def small_call(kernel, shapes, name, *args, scratch=()):
    in_specs = [ANY if isinstance(v, tuple) else VMEM for v in args]
    args = [v[0] if isinstance(v, tuple) else v for v in args]
    return pl.pallas_call(
        kernel,
        in_specs=in_specs,
        out_specs=[VMEM] * len(shapes),
        out_shape=[jax.ShapeDtypeStruct(*v) for v in shapes],
        scratch_shapes=[pltpu.VMEM(*v) for v in scratch],
        compiler_params=pltpu.CompilerParams(vmem_limit_bytes=4 * MIB),
        name=name,
    )(*args)


def widest(cuts):
    return max(b - a for a, b in zip(cuts, cuts[1:]))


def prepare(prompt_len, bits, gain, embed, x, token, cols, block):
    seqs, length, width = x.shape
    kept = length - MIN_PROMPT
    rows = seqs * kept
    shapes = [
        ((seqs, kept, 128), jnp.float32),
        ((rows, cols // 2), jnp.bfloat16),
        ((rows, cols // 2), jnp.bfloat16),
        (embed.shape, jnp.float32),
        ((rows, 128), jnp.float32),
        ((rows, block), jnp.bfloat16),
        ((seqs, length, cols), jnp.float32),
    ]
    return pl.pallas_call(
        functools.partial(prepare_kernel, 0),
        in_specs=[VMEM] * 5 + [ANY],
        out_specs=[VMEM] * len(shapes),
        out_shape=[jax.ShapeDtypeStruct(*s) for s in shapes],
        compiler_params=pltpu.CompilerParams(vmem_limit_bytes=8 * MIB),
        name="prepare",
    )(*[in_vmem(v) for v in (prompt_len, bits, gain, embed, x)], token)


def main_first(normed, common, token, sq, cuts):
    mask, gain, embed, x, w = common
    rows, cols = normed.shape[0], w.shape[1]
    scratch = pltpu.VMEM((rows, widest(cuts)), jnp.bfloat16)
    return pl.pallas_call(
        functools.partial(y_kernel, cuts),
        in_specs=[VMEM] * 6 + [ANY, VMEM],
        out_specs=[VMEM] * 2,
        out_shape=[jax.ShapeDtypeStruct((rows, cols), jnp.float32), jax.ShapeDtypeStruct(sq.shape, jnp.float32)],
        input_output_aliases={7: 1},
        scratch_shapes=[scratch, scratch],
        compiler_params=pltpu.CompilerParams(vmem_limit_bytes=12 * MIB),
        cost_estimate=cost(rows, cols, cuts),
        name="main_y",
    )(normed, mask, gain, embed, in_vmem(x), in_vmem(w), token, sq)


def main_part(kernel, name, cuts, common, token, state, extra, extra_specs, shapes, out_specs, scratch=()):
    mask, gain, embed, x, w = common
    rows, cols = state[0].shape
    shapes = [(state[0].shape, jnp.float32), (state[1].shape, jnp.float32), *shapes]
    normed = pltpu.VMEM((rows, widest(cuts)), jnp.bfloat16)
    out = pl.pallas_call(
        functools.partial(kernel, cuts),
        in_specs=[VMEM] * 5 + [ANY] + [VMEM] * 2 + extra_specs,
        out_specs=[VMEM] * 2 + out_specs,
        out_shape=[jax.ShapeDtypeStruct(*s) for s in shapes],
        input_output_aliases={6: 0, 7: 1},
        scratch_shapes=[normed, normed, *scratch],
        compiler_params=pltpu.CompilerParams(vmem_limit_bytes=12 * MIB),
        cost_estimate=cost(rows, cols, cuts),
        name=name,
    )(mask, gain, embed, in_vmem(x), in_vmem(w), token, *state, *extra)
    return out[:2], out[2:]


def add_kernel(mine_ref, theirs_ref, *refs):
    refs[-1][...] = (mine_ref[...].astype(jnp.float32) + theirs_ref[...].astype(jnp.float32)).astype(jnp.bfloat16)


def gather_sum_kernel(mine_ref, r1_ref, r2_ref, r3_ref, _, total_ref, sent_ref):
    total = mine_ref[...] + r1_ref[...].astype(jnp.float32)
    total += r2_ref[...].astype(jnp.float32) + r3_ref[...].astype(jnp.float32)
    total_ref[...] = total
    sent_ref[...] = total.astype(jnp.bfloat16)


def parity():
    return lax.rem(lax.axis_index("y"), 2)


def by_parity(v):
    groups = v.reshape(v.shape[0] // 16, 2, 8, v.shape[1])
    flat = (v.shape[0] // 2, v.shape[1])
    even = parity() == 0
    mine = jnp.where(even, groups[:, 0], groups[:, 1])
    others = jnp.where(even, groups[:, 1], groups[:, 0])
    return mine.reshape(flat), others.reshape(flat)


def from_parity(mine, others):
    shape = (mine.shape[0] // 8, 8, mine.shape[1])
    even = parity() == 0
    mine, others = mine.reshape(shape), others.reshape(shape)
    groups = jnp.stack([jnp.where(even, mine, others), jnp.where(even, others, mine)], axis=1)
    return groups.reshape(2 * shape[0] * 8, shape[2])


def core_sum_kernel(mine_ref, theirs_ref, total_ref, same_ref, flip_ref):
    a = mine_ref[0] + theirs_ref[0].astype(jnp.float32)
    b = mine_ref[1] + theirs_ref[1].astype(jnp.float32)
    mine, others = by_parity(a)
    total = jnp.concatenate([b, mine], axis=0)
    total_ref[...] = total
    same_ref[...] = total.astype(jnp.bfloat16)
    flip_ref[...] = jnp.concatenate([b, others], axis=0).astype(jnp.bfloat16)


def update_kernel(total_ref, theirs_ref, factors_ref, first_ref, second_ref, _, a_ref, b_ref, rows_ref, sum_ref):
    rank, width = b_ref.shape
    at = core_lanes(width)
    total = total_ref[...] + theirs_ref[...].astype(jnp.float32)
    first, second = adam_update(total[:rank], first_ref[1, :, at], second_ref[1, :, at])
    b_ref[...] = factor_update(first, second, factors_ref[1, :, at]).astype(jnp.bfloat16)
    mine = [by_parity(ref[0, :, at])[0] for ref in (factors_ref, first_ref, second_ref)]
    first, second = adam_update(total[rank:], mine[1], mine[2])
    a_ref[...] = factor_update(first, second, mine[0]).astype(jnp.bfloat16)
    sum_ref[...] = total
    group = lax.axis_index("zh") * 2 + lax.axis_index("y") // 2
    rows_ref[0] = sum_ref[pl.ds(pl.multiple_of(rank + group * 8, 8), 8)]
    rows_ref[1] = sum_ref[chip_rows()]


ROW_BY_ROW = (((1,), (1,)), ((), ()))


def low_rank_first_kernel(own_ref, mine_ref, out_ref):
    out_ref[...] = lax.dot_general(own_ref[...], mine_ref[...], ROW_BY_ROW, preferred_element_type=jnp.float32)


def low_rank_kernel(first_ref, own_ref, other_ref, out_ref):
    rows, rank = first_ref.shape
    half = out_ref.shape[0]
    prod = lax.dot_general(own_ref[...], other_ref[...], ROW_BY_ROW, preferred_element_type=jnp.float32)
    prod += first_ref[...]
    tail = jnp.concatenate([prod[half:], jnp.zeros((2 * half - rows, rank), jnp.float32)], axis=0)
    out_ref[...] = jnp.concatenate([prod[:half], tail], axis=1).astype(jnp.bfloat16)


def pair_kernel(mine_ref, other_ref, _, out_ref):
    out_ref[...] = jnp.concatenate([mine_ref[...], other_ref[...]], axis=0)


def join_kernel(here_ref, there_ref, _, a_ref):
    here, there = here_ref[...].astype(jnp.float32), there_ref[...].astype(jnp.float32)
    half = here.shape[0] // 2
    mine, other = from_parity(here[:half], there[:half]), from_parity(here[half:], there[half:])
    even = lax.axis_index("c") == 0
    joined = jnp.concatenate([jnp.where(even, mine, other), jnp.where(even, other, mine)], axis=1)
    a_ref[...] = joined.astype(jnp.bfloat16)


def final_kernel(
    mine_ref, r1_ref, r2_ref, r3_ref, a_ref, rest_ref, acc_ref, scale_ref, first_ref, second_ref,
    out_ref, first_out, second_out, stage_ref, sems, moment_sems,
):
    copies = [
        pltpu.make_async_copy(first_ref, first_out, moment_sems.at[0]),
        pltpu.make_async_copy(second_ref, second_out, moment_sems.at[1]),
    ]
    start(copies)
    seqs, length, cols = rest_ref.shape
    kept = length - MIN_PROMPT
    rank = a_ref.shape[0]
    half = mine_ref.shape[0]
    total = mine_ref[...].astype(jnp.float32) + r1_ref[...].astype(jnp.float32)
    total += r2_ref[...].astype(jnp.float32) + r3_ref[...].astype(jnp.float32)
    low = jnp.concatenate([total[:, :rank], total[: seqs * kept - half, rank:]], axis=0)
    low = (low * (adapter_scale * scale_ref[:, :rank])).astype(jnp.bfloat16)
    a = a_ref[...]
    for seq in range(seqs):
        adapter = jnp.dot(low[seq * kept : (seq + 1) * kept], a, preferred_element_type=jnp.float32)
        for piece in range(length // PIECE):
            begin, end = piece * PIECE, (piece + 1) * PIECE
            lead = max(MIN_PROMPT - begin, 0)
            own = slice(begin + lead - MIN_PROMPT, end - MIN_PROMPT)
            rows = slice(seq * kept + own.start, seq * kept + own.stop)
            for j in range(cols // 128):
                lanes = slice(j * 128, (j + 1) * 128)
                value = rest_ref[seq, begin + lead : end, lanes] + scale_ref[rows] * acc_ref[rows, lanes]
                value += adapter[own, lanes]
                if lead:
                    value = jnp.concatenate([rest_ref[seq, begin : begin + lead, lanes], value], axis=0)
                stage_ref[seq, begin:end, lanes] = value.astype(jnp.bfloat16)
            at = pl.ds(begin, PIECE)
            copy = pltpu.make_async_copy(stage_ref.at[seq, at], out_ref.at[seq, at], sems.at[seq, piece])
            copy.start()
            copies.append(copy)
    wait(copies)


def final(mine, received, a, rest, acc, scale, moments):
    return pl.pallas_call(
        final_kernel,
        in_specs=[VMEM] * 10,
        out_specs=[HBM] * 3,
        out_shape=[
            jax.ShapeDtypeStruct(rest.shape, jnp.bfloat16),
            *[jax.ShapeDtypeStruct(v.shape, jnp.float32) for v in moments],
        ],
        scratch_shapes=[
            pltpu.VMEM(rest.shape, jnp.bfloat16),
            pltpu.SemaphoreType.DMA((rest.shape[0], rest.shape[1] // PIECE)),
            pltpu.SemaphoreType.DMA((2,)),
        ],
        compiler_params=pltpu.CompilerParams(vmem_limit_bytes=16 * MIB),
        name="final",
    )(mine, *received, a, rest, acc, scale, *moments)


def local(x, mask_bits, prompt_len, weight, norm_gain, mask_embed, grads, factors, first_moment, second_moment):
    width = x.shape[2]
    cols = weight.shape[1]
    two, rank, _ = factors.shape
    wide, narrow = jnp.float32, jnp.bfloat16
    gain = norm_gain.reshape(width // 128, 128)
    embed = mask_embed.reshape(width // 128, 128)

    own, outgoing = pack(grads)
    from_core = exchange(outgoing, "c", (1,))
    held = (rank + rank // 2, cols // 2)
    total, same, flip = small_call(
        core_sum_kernel, [(held, wide), (held, narrow), (held, narrow)], "sum_c", own, from_core
    )
    from_y = [exchange(v, "y", (k,)) for v, k in ((flip, 1), (flip, 3), (same, 2))]

    mask, own_mine, own_other, embed, sq, normed, rest = prepare(
        prompt_len.reshape(1, -1), mask_bits, gain, embed, x, same, cols, CUTS[0][1]
    )
    common = (mask, gain, embed, x, weight)
    state = main_first(normed, common, same, sq, CUTS[0])
    total, sent = small_call(
        gather_sum_kernel, [(held, wide), (held, narrow)], "sum_y", total, *from_y, (state[1],)
    )
    from_z = exchange(sent, ("zh",), (1,))
    state, _ = main_part(part_kernel, "main_z", CUTS[1], common, sent, state, [], [], [], [])

    params = [in_vmem(v) for v in (factors, first_moment, second_moment)]
    part = (rank, cols // 2)
    half_part = (rank // 2, cols // 2)
    a_half, b_own, rows_own = small_call(
        update_kernel, [(half_part, narrow), (part, narrow), ((two, 8, cols // 2), wide)],
        "update", total, from_z, *params, (state[1],), scratch=[(held, wide)],
    )
    b_other = exchange(b_own, "c", (1,))
    a_core = exchange(a_half, "c", (1,))
    rows_other = exchange(rows_own, "c", (1,))
    rows = own_mine.shape[0]
    (low,) = small_call(low_rank_first_kernel, [((rows, rank), wide)], "low_rank_first", own_mine, b_own)
    packed = (-(-rows // 32) * 16, 2 * rank)
    (low,) = small_call(low_rank_kernel, [(packed, narrow)], "low_rank", low, own_other, b_other)
    from_zl = exchange(low, ("zl",), (1,))
    (a_here,) = small_call(pair_kernel, [(part, narrow)], "pair_a", a_half, a_core, (low,))
    a_there = exchange(a_here, "y", (1,))
    state, _ = main_part(part_kernel, "main_zl", CUTS[2], common, low, state, [], [], [], [])
    (low,) = small_call(add_kernel, [(low.shape, narrow)], "sum_zl", low, from_zl, (state[1],))
    from_x = [exchange(low, ("x",), (k,)) for k in (1, 3, 2)]
    four = ((two, 4, cols), wide)
    state, (scale, *moments) = main_part(
        last_kernel, "main_x", CUTS[3], common, low, state, [rows_own, rows_other, *params[1:]], [VMEM] * 4,
        [(state[1].shape, wide), four, four], [VMEM] * 3,
    )
    (a,) = small_call(join_kernel, [((rank, cols), narrow)], "join_a", a_here, a_there, (scale,))
    return final(low, from_x, a, rest, state[0], scale, moments)


def solution(mesh):
    split = Mesh(mesh.devices.reshape(2, 4, 2, 4, 2), ("zh", "y", "c", "x", "zl"))
    placed = (
        P(DP, None, None),
        P(DP, None),
        P(DP),
        P(None, TENSOR),
        P(),
        P(),
        P(DP, None, None, TENSOR),
        P(None, None, TENSOR),
        P(None, None, TENSOR),
        P(None, None, TENSOR),
    )
    return jax.shard_map(
        local,
        mesh=split,
        in_specs=placed,
        out_specs=(P(DP, None, TENSOR), P(None, DP, TENSOR), P(None, DP, TENSOR)),
        check_vma=False,
    )
```
